256 devices in a mesh: ctx: 128 (over y_lo, z, x, core), tp: 2 (over y_hi).
Axes of the slice: x: 4, y: 4 (y_hi: 2, y_lo: 2; y = y_hi * 2 + y_lo), z: 8, core: 2. Of those that a mesh axis runs over, the one named last changes fastest.
Arguments:
- audio_feats: bfloat16 [2, 65536, 512], P('tp', 'ctx'), may hold values from -6 to 6
- res_conv: bfloat16 [2, 3, 512, 256], P('tp'), may hold values from -0.15625 to 0.15625
- res_out: bfloat16 [2, 256, 512], P('tp'), may hold values from -0.375 to 0.375
- down_conv: bfloat16 [2, 4, 512, 512], P('tp'), may hold values from -0.125 to 0.125
- stream_embed: bfloat16 [2, 512, 4096], P('tp'), may hold values from -0.25 to 0.25
- turn_lengths: int32 [2, 32], replicated, may hold values from 1 to 4096, 32768 in all within a row
- speaker_table: float32 [2, 4096], replicated, may hold values from -6 to 6
- norm_gain: float32 [4096], replicated, may hold values from 0.25 to 1.75
- qkv_weight: bfloat16 [3, 4096, 2048], P(None, 'ctx', 'tp')
Outputs:
- embedded: bfloat16 [32768, 4096], P('ctx', 'tp')
- attended: bfloat16 [32768, 2048], P('ctx', 'tp')
The draws below stay inside these ranges and needn't reach their ends.
Inputs may be any that keep to these rules, and one draw needn't show every extreme that they name: `turn_lengths`: each row holds the 32 turn lengths of one stream; they sum to 32768 and the longest is exactly 4096.
All inputs are finite; a program needn't handle non-finite values.
Results may differ from the reference program's by a relative error of at most 0.0085.
Values may be sent and summed in bfloat16 or wider, within the bound.
No kernel may reach another device: no remote copies, remote signals or barrier semaphores. Data moves between devices by JAX's collectives and lax.ppermute only.
A program may use at most 128 MiB of HBM per device.

```python
import math
import jax
import jax.numpy as jnp
import numpy as np
from jax import lax

D = 4096
CH = 512
HID = 256
HEADS = 16
HD = 128
FRAME_DEV = 256
LAGS = 7
TURNS = 32
FRAMES = 32768
SAMPLES = 65536
N_CTX = 128


def draw_qkv_weight(key, part):
    key = jax.random.fold_in(key, 11)
    cols = HEADS * HD
    weight = jax.random.normal(key, (3, D, cols), jnp.float32) * D ** (-0.5)
    return weight.astype(jnp.bfloat16)


def levels(key, dims, cuts, least, high):
    def one(position, blocks):
        steps = jax.random.uniform(jax.random.fold_in(jax.random.fold_in(key, 6), position), (blocks,), jnp.float32, least / len(cuts), high / len(cuts))
        return jnp.repeat(jnp.exp(steps), dims[position] // blocks).reshape((-1,) + (1,) * (len(dims) - position - 1))

    loudness = one(*cuts[0])
    for cut in cuts[1:]:
        loudness = loudness * one(*cut)
    return loudness


def length_profile(amount, total, bound, skew):
    weights = [(1 << 20) // math.isqrt(standing ** skew) + 1 for standing in range(2, amount + 1)]
    rest, counts = total - bound - (amount - 1), [1] * (amount - 1)
    while rest > 0:
        free = [i for i in range(amount - 1) if counts[i] < bound]
        mass, budget = sum([weights[i] for i in free]), rest
        for i in free:
            more = min(bound - counts[i], max(1, budget * weights[i] // mass), rest)
            counts[i] = counts[i] + more
            rest = rest - more
    return np.array([bound] + counts)


def ragged_sizes(key, amount, total, limit, lean):
    if amount == 2:
        one = jax.random.randint(key, (), max(1, total - limit), min(limit, total - 1) + 1)
        return jnp.stack([one, total - one])
    tallies = jnp.asarray(length_profile(amount, total, limit, lean), jnp.int32)
    couples = (amount - 1) // 2
    donor, taker = tallies[1:1 + 2 * couples:2], tallies[2:2 + 2 * couples:2]
    margin = jnp.minimum(donor - 1, limit - taker)
    shifted = jax.random.randint(jax.random.fold_in(key, 1), (couples,), 0, 1 << 20) % (margin + 1)
    tallies = tallies.at[1:1 + 2 * couples:2].set(donor - shifted).at[2:2 + 2 * couples:2].set(taker + shifted)
    return tallies[jax.random.permutation(jax.random.fold_in(key, 2), amount)]


def bell_draw(stream_key, dims, scale, reach, cuts=(), kind=jnp.bfloat16):
    result = jax.random.normal(stream_key, dims, jnp.float32) * scale
    if len(cuts) > 0:
        result = levels(stream_key, dims, cuts, -0.22, 0.18) * result
    return jnp.clip(result, min=-reach, max=reach).astype(kind)


def setup_inputs(seed: int = 0) -> dict:
    key_list = jax.random.split(jax.random.key(seed), 10)
    return {
        "audio_feats": bell_draw(key_list[0], (2, SAMPLES, CH), 1.0, 6.0, ((0, 2), (1, 128))),
        "res_conv": bell_draw(key_list[1], (2, 3, CH, HID), (3 * CH) ** -0.5, 0.15625, ((0, 2),)),
        "res_out": bell_draw(key_list[2], (2, HID, CH), HID ** -0.5, 0.375, ((0, 2),)),
        "down_conv": bell_draw(key_list[3], (2, 4, CH, CH), (4 * CH) ** -0.5, 0.125, ((0, 2),)),
        "stream_embed": bell_draw(key_list[4], (2, CH, D), CH ** -0.5, 0.25, ((0, 2),)),
        "turn_lengths": jax.vmap(lambda own: ragged_sizes(own, TURNS, FRAMES, FRAMES // 8, 2))(jax.random.split(key_list[5], 2)).reshape((2, TURNS)).astype(jnp.int32),
        "speaker_table": bell_draw(key_list[6], (2, D), 1.0, 6.0, (), jnp.float32),
        "norm_gain": jnp.clip(1.0 + 0.15 * jax.random.normal(key_list[7], (D,), jnp.float32), 0.25, 1.75),
        "qkv_weight": draw_qkv_weight(jax.random.fold_in(key_list[9], 71), 0),
    }


def elu_act(values):
    return jax.nn.elu(values.astype(jnp.float32))

def encode(audio, conv_taps, conv_back, conv_down):
    steps = audio.shape[0]
    channels = audio.shape[1]
    inputs = elu_act(audio).astype(jnp.bfloat16)
    padded = jnp.pad(inputs, ((6, 0), (0, 0)))
    stacked = jnp.concatenate([padded[0:steps], padded[3:3 + steps], padded[6:6 + steps]], axis=1)
    inner = jnp.dot(stacked, conv_taps.reshape(3 * channels, conv_taps.shape[2]), preferred_element_type=jnp.float32)
    hidden = elu_act(inner).astype(jnp.bfloat16)
    resid = (audio.astype(jnp.float32) + jnp.dot(hidden, conv_back, preferred_element_type=jnp.float32)).astype(jnp.bfloat16)
    activ = elu_act(resid).astype(jnp.bfloat16)
    widened = jnp.pad(activ, ((2, 0), (0, 0)))
    frames = steps // 2
    first = widened[:2 * frames].reshape(frames, 2 * channels)
    second = widened[2:2 * frames + 2].reshape(frames, 2 * channels)
    stacked = jnp.concatenate([first, second], axis=1)
    return jnp.dot(stacked, conv_down.reshape(4 * channels, channels), preferred_element_type=jnp.float32).astype(jnp.bfloat16)

def reference(audio_feats, res_conv, res_out, down_conv, stream_embed, turn_lengths, speaker_table, norm_gain, qkv_weight):
    latent_a = encode(audio_feats[0], res_conv[0], res_out[0], down_conv[0])
    latent_b = encode(audio_feats[1], res_conv[1], res_out[1], down_conv[1])
    summed = jnp.dot(latent_a, stream_embed[0], preferred_element_type=jnp.float32) + jnp.dot(latent_b, stream_embed[1], preferred_element_type=jnp.float32)
    positions = jnp.arange(FRAMES, dtype=jnp.int32)
    bounds = jnp.cumsum(turn_lengths, axis=1).astype(jnp.int32)
    turn = lax.optimization_barrier(jnp.sum((bounds[:, :, None] <= positions[None, None, :]).astype(jnp.int32), axis=1))
    active = (turn % 2 == 1).astype(jnp.float32)
    x_full = summed + active[0][:, None] * speaker_table[0][None, :] + active[1][:, None] * speaker_table[1][None, :]
    embedded = x_full.astype(jnp.bfloat16)
    meansq = lax.optimization_barrier(jnp.mean(x_full * x_full, axis=1))
    normed = (x_full * lax.rsqrt(meansq + 1e-05)[:, None] * norm_gain[None, :]).astype(jnp.bfloat16)
    query = jnp.dot(normed, qkv_weight[0], preferred_element_type=jnp.float32).astype(jnp.bfloat16)
    keys = jnp.dot(normed, qkv_weight[1], preferred_element_type=jnp.float32).astype(jnp.bfloat16)
    values = jnp.dot(normed, qkv_weight[2], preferred_element_type=jnp.float32).astype(jnp.bfloat16)
    block = FRAME_DEV
    span = (LAGS + 1) * block
    keys_pad = jnp.pad(keys, ((LAGS * block, 0), (0, 0)))
    values_pad = jnp.pad(values, ((LAGS * block, 0), (0, 0)))
    scale = 1.0 / HD ** 0.5

    def one_block(index):
        start = (index * block).astype(jnp.int32)
        qblock = lax.dynamic_slice_in_dim(query, start, block, 0).reshape(block, HEADS, HD).astype(jnp.float32)
        kblock = lax.dynamic_slice_in_dim(keys_pad, start, span, 0).reshape(span, HEADS, HD).astype(jnp.float32)
        vblock = lax.dynamic_slice_in_dim(values_pad, start, span, 0).reshape(span, HEADS, HD).astype(jnp.float32)
        scores = jnp.einsum('qhd,khd->hqk', qblock, kblock, precision=lax.Precision.HIGHEST) * scale
        rows = jnp.arange(block, dtype=jnp.int32)[:, None]
        cols = jnp.arange(span, dtype=jnp.int32)[None, :]
        diff = LAGS * block + rows - cols
        keypos = (index - LAGS) * block + cols
        allowed = (diff >= 0) & (diff < LAGS * block) & (keypos >= 0)
        scores = jnp.where(allowed[None], scores, -1e+30)
        top = lax.optimization_barrier(jnp.max(scores, axis=-1, keepdims=True))
        expo = jnp.exp(scores - top)
        weights = (expo / lax.optimization_barrier(jnp.sum(expo, axis=-1, keepdims=True))).astype(jnp.bfloat16)
        out = jnp.einsum('hqk,khd->qhd', weights.astype(jnp.float32), vblock, precision=lax.Precision.HIGHEST)
        return out.astype(jnp.bfloat16).reshape(block, HEADS * HD)
    attended = lax.map(one_block, jnp.arange(N_CTX, dtype=jnp.int32)).reshape(FRAMES, HEADS * HD)
    return (embedded, attended)
```

```python
import functools

import jax
import jax.numpy as jnp
from jax import lax
from jax.experimental import pallas as pl
from jax.experimental.pallas import tpu as pltpu
from jax.sharding import Mesh, PartitionSpec as P

HD = 128
BLOCK = 256
LAGS = 7
D = 4096
CH = 512
CTX = ("yl", "z", "x", "c")
ROW = ("x", "c")
SWAP = [(0, 1), (1, 0)]
BF = jnp.bfloat16
F32 = jnp.float32


def elu(v):
    return jnp.where(v > 0, v, jnp.exp(jnp.minimum(v, 0.0)) - 1.0)


def dot(a, b):
    return jnp.dot(a, b, preferred_element_type=F32)


def encoder(ext, conv_taps, conv_back, conv_down):
    wide = ext.astype(F32)
    u = elu(wide).astype(BF)
    rows = ext.shape[0] - 6
    inner = (
        dot(u[0:rows], conv_taps[0]) + dot(u[3 : 3 + rows], conv_taps[1]) + dot(u[6 : 6 + rows], conv_taps[2])
    )
    hidden = elu(inner).astype(BF)
    resid = (wide[6:] + dot(hidden, conv_back)).astype(BF)
    act = elu(resid.astype(F32)).astype(BF)
    pairs = act.reshape(rows // 2, 2 * CH)
    taps = conv_down.reshape(2, 2 * CH, CH)
    return (dot(pairs[:-1], taps[0]) + dot(pairs[1:], taps[1])).astype(BF)


def attention_kernel(first_ref, q_ref, k_ref, v_ref, o_ref):
    block = pl.program_id(0)
    start = pl.multiple_of((block + 1) * BLOCK, BLOCK)
    span = (LAGS + 1) * BLOCK
    q = q_ref[...]
    k = k_ref[pl.ds(start, span), :]
    s = lax.dot_general(q, k, (((1,), (1,)), ((), ())), preferred_element_type=F32)
    rows = lax.broadcasted_iota(jnp.int32, (BLOCK, span), 0)
    cols = lax.broadcasted_iota(jnp.int32, (BLOCK, span), 1)
    diff = LAGS * BLOCK + rows - cols
    least = jnp.where(first_ref[0] == 1, (LAGS - block) * BLOCK, 0)
    allowed = (diff >= 0) & (diff < LAGS * BLOCK) & (cols >= least)
    s = jnp.where(allowed, s, -1e30)
    top = jnp.max(s, axis=-1, keepdims=True)
    p = jnp.exp(s - top)
    total = jnp.sum(p, axis=-1, keepdims=True)
    o = dot(p.astype(BF), v_ref[pl.ds(start, span), :])
    o_ref[...] = (o / total).astype(BF)


def attention(first, q, k, v):
    rows = q.shape[0]
    return pl.pallas_call(
        attention_kernel,
        grid=(rows // BLOCK,),
        in_specs=[
            pl.BlockSpec(memory_space=pltpu.SMEM),
            pl.BlockSpec((BLOCK, HD), lambda i: (i, 0)),
            pl.BlockSpec(k.shape, lambda i: (0, 0)),
            pl.BlockSpec(v.shape, lambda i: (0, 0)),
        ],
        out_specs=pl.BlockSpec((BLOCK, HD), lambda i: (i, 0)),
        out_shape=jax.ShapeDtypeStruct(q.shape, BF),
        compiler_params=pltpu.CompilerParams(vmem_limit_bytes=40 * 1024 * 1024),
        cost_estimate=pl.CostEstimate(flops=4 * rows * 2048 * HD, bytes_accessed=4 * rows * HD * 2, transcendentals=rows * 2048),
    )(first, q, k, v)


def head_weights(stream_embed, speaker_table, norm_gain, qkv_weight):
    yl = lax.axis_index("yl")
    z = lax.axis_index("z")
    w = lax.all_to_all(qkv_weight, ROW, 2, 1, tiled=True)
    w = lax.all_gather(w, "yl", axis=0)
    w = w.transpose(0, 2, 1, 3).reshape(512, 3 * HD)

    def of_z(a):
        a = a.reshape(a.shape[:-1] + (2, 8, 256))
        a = lax.dynamic_index_in_dim(a, z, a.ndim - 2, keepdims=False)
        return a.reshape(a.shape[:-2] + (512,))

    gain = of_z(norm_gain)
    mine = of_z(lax.dynamic_slice_in_dim(stream_embed, yl * 256, 256, 0))
    rest = lax.ppermute(mine, "tp", SWAP)
    embed = (jnp.concatenate([mine, rest], axis=0).astype(F32) * gain).astype(BF)
    table = of_z(speaker_table) * gain
    high = table.astype(BF)
    low = (table - high.astype(F32)).astype(BF)
    part = dot(embed, w).astype(BF).reshape(8, 64, 3 * HD)
    line = dot(high, w) + dot(low, w)
    top = line.astype(BF)
    rem = (line - top.astype(F32)).astype(BF)
    tail = jnp.concatenate([top, rem, jnp.zeros((12, 3 * HD), BF)], axis=0)
    packed = jnp.concatenate([part, jnp.broadcast_to(tail[None], (8, 16, 3 * HD))], axis=1)
    packed = lax.all_to_all(packed, "z", 0, 0, tiled=True)
    total = jnp.sum(packed.astype(F32), axis=0)
    lines = total[64:66] + total[66:68]
    m = lax.all_gather(total[:64].astype(BF), "z", axis=0, tiled=True)
    m = lax.all_gather(m, "yl", axis=0)
    m = m.reshape(2, 2, 256, 3 * HD).transpose(1, 0, 2, 3).reshape(2 * CH, 3 * HD)
    return m, lines


def on_device(
    audio_feats,
    res_conv,
    res_out,
    down_conv,
    stream_embed,
    turn_lengths,
    speaker_table,
    norm_gain,
    qkv_weight,
):
    tp = lax.axis_index("tp")
    row = lax.axis_index("yl") * 8 + lax.axis_index("z")
    audio = audio_feats[0]
    halo = lax.ppermute(audio[-8:], CTX, [(i, i + 1) for i in range(127)])
    latent = encoder(jnp.concatenate([halo, audio], axis=0), res_conv[0], res_out[0], down_conv[0])
    other = lax.ppermute(latent, "tp", SWAP)
    y = jnp.concatenate([latent, other], axis=1)
    behind = [(i, i + 1) for i in range(15)]
    prev = lax.ppermute(y, ("yl", "z"), behind)
    both = jnp.stack([prev, y])
    every = lax.all_gather(both, ROW, axis=1)
    every = every.reshape(16 * BLOCK, 2 * CH)

    m, lines = head_weights(stream_embed[0], speaker_table, norm_gain, qkv_weight)

    bounds = jnp.cumsum(turn_lengths, axis=1)
    frames = (row - 1) * 8 * BLOCK + jnp.arange(16 * BLOCK, dtype=jnp.int32)
    turn = jnp.sum((bounds[:, None, :] <= frames[None, :, None]).astype(jnp.int32), axis=2)
    active = (turn % 2 == 1).astype(F32)
    here = 8 * BLOCK + (lax.axis_index("x") * 2 + lax.axis_index("c")) * BLOCK
    active_here = lax.dynamic_slice_in_dim(active, here, BLOCK, 1)

    embed = stream_embed[0].reshape(CH, 2, D // 2)
    own = dot(latent, lax.dynamic_index_in_dim(embed, tp, 1, keepdims=False))
    give = dot(latent, lax.dynamic_index_in_dim(embed, 1 - tp, 1, keepdims=False)).astype(BF)
    got = lax.ppermute(give, "tp", SWAP)
    table = lax.dynamic_slice_in_dim(speaker_table, tp * (D // 2), D // 2, 1)
    x = own + got.astype(F32) + active_here[0][:, None] * table[0] + active_here[1][:, None] * table[1]
    embedded = x.astype(BF)
    square = jnp.sum(x * x, axis=1)
    square = square + lax.ppermute(square, "tp", SWAP)
    scale = lax.rsqrt(square * (1.0 / D) + 1e-05)
    scale_prev = lax.ppermute(scale, ("yl", "z"), behind)
    scales = lax.all_gather(jnp.stack([scale_prev, scale]), ROW, axis=1).reshape(16 * BLOCK, 1)

    def project(rows, weight, line, act, factor):
        extra = act[0][:, None] * line[0] + act[1][:, None] * line[1]
        return ((dot(rows, weight) + extra) * factor).astype(BF)

    q = project(every[8 * BLOCK :], m[:, :HD], lines[:, :HD], active[:, 8 * BLOCK :], scales[8 * BLOCK :] * HD**-0.5)
    kv = project(every, m[:, HD:], lines[:, HD:], active, scales)
    first = (row == 0).astype(jnp.int32).reshape(1)
    out = attention(first, q, kv[:, :HD], kv[:, HD:])
    attended = lax.all_to_all(out, ROW, 0, 1, tiled=True)
    return embedded, attended


def solution(mesh):
    fine = Mesh(mesh.devices.reshape(2, 8, 4, 2, 2), CTX + ("tp",))
    placed = (
        P("tp", CTX, None),
        P("tp", None, None, None),
        P("tp", None, None),
        P("tp", None, None, None),
        P("tp", None, None),
        P(),
        P(),
        P(),
        P(None, CTX, "tp"),
    )
    return jax.shard_map(
        on_device,
        mesh=fine,
        in_specs=placed,
        out_specs=(P(CTX, "tp"), P(CTX, "tp")),
        check_vma=False,
    )
```

```python
import functools

import jax
import jax.numpy as jnp
from jax import lax
from jax.experimental import pallas as pl
from jax.experimental.pallas import tpu as pltpu
from jax.sharding import Mesh, PartitionSpec as P

HD = 128
BLOCK = 256
D = 4096
CH = 512
CTX = ("yl", "z", "x", "c")
SWAP = [(0, 1), (1, 0)]
BF = jnp.bfloat16
F32 = jnp.float32
VMEM_LIMIT = 48 * 1024 * 1024
LOG2E = 1.4426950408889634


def elu(v):
    return jnp.where(v > 0, v, jnp.exp(jnp.minimum(v, 0.0)) - 1.0)


def dot(a, b):
    return jnp.dot(a, b, preferred_element_type=F32)


def in_vmem(n):
    return [pl.BlockSpec(memory_space=pltpu.VMEM)] * n


def params():
    return pltpu.CompilerParams(vmem_limit_bytes=VMEM_LIMIT)


def encoder_kernel(halo_ref, audio_ref, taps_ref, back_ref, down_ref, out_ref, u_ref, e_ref):
    u_ref[0:8, :] = jnp.zeros((8, CH), F32)
    u_ref[8:16, :] = elu(halo_ref[...].astype(F32))
    u_ref[16:, :] = elu(audio_ref[...].astype(F32))
    rows = audio_ref.shape[0] + 8
    inner = dot(u_ref[2 : 2 + rows, :].astype(BF), taps_ref[0])
    inner += dot(u_ref[5 : 5 + rows, :].astype(BF), taps_ref[1])
    inner += dot(u_ref[8 : 8 + rows, :].astype(BF), taps_ref[2])
    hidden = elu(inner).astype(BF)
    branch = dot(hidden, back_ref[...])
    first = (halo_ref[...].astype(F32) + branch[0:8]).astype(BF)
    first = elu(first.astype(F32)).astype(BF).astype(F32)
    rest = (audio_ref[...].astype(F32) + branch[8:]).astype(BF)
    rest = elu(rest.astype(F32)).astype(BF).astype(F32)
    for j in range(CH // 128):
        e_ref[j, 0:8, :] = first[:, j * 128 : (j + 1) * 128]
        e_ref[j, 8:, :] = rest[:, j * 128 : (j + 1) * 128]
    acc = jnp.zeros((BLOCK, CH), F32)
    for k in range(4):
        e = [e_ref[j, pl.ds(6 + k, BLOCK, stride=2), :].astype(BF) for j in range(CH // 128)]
        acc += dot(jnp.concatenate(e, axis=1), down_ref[k])
    out_ref[...] = acc.astype(BF)


def encoder(halo, audio, taps, back, down):
    return pl.pallas_call(
        encoder_kernel,
        in_specs=in_vmem(5),
        out_specs=pl.BlockSpec(memory_space=pltpu.VMEM),
        out_shape=jax.ShapeDtypeStruct((BLOCK, CH), BF),
        scratch_shapes=[pltpu.VMEM((528, CH), F32), pltpu.VMEM((CH // 128, 520, 128), F32)],
        compiler_params=params(),
        cost_estimate=pl.CostEstimate(flops=1100000000, bytes_accessed=4 << 20, transcendentals=600000),
    )(halo, audio, taps, back, down)


def partial_kernel(w_ref, mine_ref, rest_ref, gain_ref, table_ref, out_ref):
    part = None
    line = None
    for y in range(2):
        w = jnp.concatenate(
            [
                jnp.concatenate([w_ref[c, y, x, j] for x in range(4) for c in range(2)], axis=0)
                for j in range(3)
            ],
            axis=1,
        )
        gain = gain_ref[y]
        embed = jnp.concatenate([mine_ref[y], rest_ref[y]], axis=0).astype(F32) * gain
        table = table_ref[y] * gain
        high = table.astype(BF)
        low = (table - high.astype(F32)).astype(BF)
        a = dot(embed.astype(BF), w)
        b = dot(high, w) + dot(low, w)
        part = a if part is None else part + a
        line = b if line is None else line + b
    top = line.astype(BF).astype(F32)
    rem = line - top
    rows = [v[s : s + 1, k * 128 : (k + 1) * 128] for v in (top, rem) for s in range(2) for k in range(6)]
    tail = jnp.concatenate(rows + [jnp.zeros((8, 128), F32)], axis=0).astype(BF)
    for i in range(8):
        out_ref[i, :, 0:768] = part[i * 32 : (i + 1) * 32].astype(BF)
        out_ref[i, :, 768:896] = tail


def head_weights(stream_embed, speaker_table, norm_gain, qkv_weight):
    yl = lax.axis_index("yl")
    z = lax.axis_index("z")
    c = lax.axis_index("c")
    w = qkv_weight.reshape(3, 32, 4, 256).transpose(2, 0, 1, 3)
    w = lax.all_to_all(w, "x", 0, 0, tiled=True)
    w = jnp.stack([w, lax.ppermute(w, "yl", SWAP)])
    w = lax.all_gather(w, "c", axis=0)

    def of_z(a):
        a = a.reshape(a.shape[0], 2, 8, 256)
        return jnp.stack(
            [lax.dynamic_slice(a, (0, y, z, 0), (a.shape[0], 1, 1, 256)).reshape(a.shape[0], 256) for y in (yl, 1 - yl)]
        )

    mine = of_z(lax.dynamic_slice_in_dim(stream_embed, (yl * 2 + c) * 128, 128, 0))
    rest = lax.ppermute(mine, "tp", SWAP)
    packed = pl.pallas_call(
        partial_kernel,
        in_specs=in_vmem(5),
        out_specs=pl.BlockSpec(memory_space=pltpu.VMEM),
        out_shape=jax.ShapeDtypeStruct((8, 32, 896), BF),
        compiler_params=params(),
        cost_estimate=pl.CostEstimate(flops=210000000, bytes_accessed=2 << 20, transcendentals=0),
    )(w, mine, rest, of_z(norm_gain[None]), of_z(jnp.pad(speaker_table, ((0, 6), (0, 0)))))
    packed = lax.all_to_all(packed, "z", 0, 0, tiled=True)
    total = jnp.sum(packed.astype(F32), axis=0)
    lines = (total[0:12, 768:] + total[12:24, 768:]).reshape(2, 768)
    m = total[:, :768].astype(BF)
    m = lax.all_to_all(jnp.broadcast_to(m[None], (8, 32, 768)), "z", 0, 0, tiled=True).reshape(256, 768)
    m = jnp.stack([m, lax.ppermute(m, "yl", SWAP)])
    return lax.all_gather(m, "c", axis=0), lines


def ring(a):
    left = lax.ppermute(a, "x", [(i, (i + 1) % 4) for i in range(4)])
    right = lax.ppermute(a, "x", [(i, (i + 3) % 4) for i in range(4)])
    return left, right


def second_hop(a, b):
    left = lax.ppermute(a, "x", [(i, (i + 1) % 4) for i in range(4)])
    right = lax.ppermute(b, "x", [(i, (i + 3) % 4) for i in range(4)])
    return left, right


def gather_latents(latent, other):
    behind = [(i, i + 1) for i in range(15)]
    a = latent
    al, ar = ring(a)
    prev_a = lax.ppermute(a, ("yl", "z"), behind)
    b = jnp.stack([other, prev_a])
    bl, br = ring(b)
    c = lax.ppermute(other, ("yl", "z"), behind)
    al2, ar2 = second_hop(al[:128], ar[128:])
    cl, cr = ring(c)
    bl2, br2 = second_hop(bl[0], br[1])
    cl2, cr2 = second_hop(cl[:128], cr[128:])
    return (a, al, ar, al2, ar2, b, bl, br, bl2, br2, c, cl, cr, cl2, cr2)


def project_kernel(with_q, place_ref, *refs):
    (a, al, ar, al2, ar2, b, bl, br, bl2, br2, c, cl, cr, cl2, cr2, m_ref, line_ref, side_ref) = refs[:18]
    outs = refs[18:]
    x = place_ref[0]
    yl = place_ref[1]

    def weight(j, s):
        pieces = []
        for y in range(2):
            at = jnp.where(yl == y, 0, 1)
            for cc in range(2):
                pieces.append(m_ref[cc, at, s * 128 : (s + 1) * 128, j * 256 : (j + 1) * 256])
        return jnp.concatenate(pieces, axis=0)

    far_a = jnp.concatenate([al2[...], ar2[...]], axis=0)
    far_c = jnp.concatenate([cl2[...], cr2[...]], axis=0)
    own = [(a[...], b[0]), (ar[...], br[0]), (far_a, bl2[...]), (al[...], bl[0])]
    prev = [(b[1], c[...]), (br[1], cr[...]), (br2[...], far_c), (bl[1], cl[...])]
    jobs = [(0, outs[1], False), (1, outs[0], True)] if with_q else [(2, outs[0], True)]
    for j, out, both in jobs:
        w0, w1 = weight(j, 0), weight(j, 1)
        line = line_ref[:, j * 256 : (j + 1) * 256]
        factor = HD**-0.5 * LOG2E if j == 0 else 1.0
        for r, blocks in ((1, own), (0, prev)) if both else ((1, own),):
            for dx in range(4):
                p, q = blocks[dx]
                at = lax.rem(x + dx, 4)
                side = side_ref[4 * r + at]
                acc = dot(p, w0) + dot(q, w1)
                acc = acc + side[:, 0:1] * line[0:1] + side[:, 1:2] * line[1:2]
                acc = acc * (side[:, 2:3] * factor)
                out[4 * r + at if both else at] = acc.astype(BF)


def project(with_q, place, pieces, m, lines, side):
    shapes = [jax.ShapeDtypeStruct((8, BLOCK, 256), BF)]
    if with_q:
        shapes.append(jax.ShapeDtypeStruct((4, BLOCK, 256), BF))
    return pl.pallas_call(
        functools.partial(project_kernel, with_q),
        in_specs=[pl.BlockSpec(memory_space=pltpu.SMEM)] + in_vmem(18),
        out_specs=in_vmem(len(shapes)),
        out_shape=shapes,
        compiler_params=params(),
        cost_estimate=pl.CostEstimate(flops=1600000000, bytes_accessed=6 << 20, transcendentals=0),
    )(place, *pieces, m, lines, side)


def attention_kernel(place_ref, q_ref, km_ref, kt_ref, vm_ref, vt_ref, o_ref):
    at = lax.rem(place_ref[0] + place_ref[3 + pl.program_id(0)], 4)
    core = place_ref[1]
    first = place_ref[2]
    rows = lax.broadcasted_iota(jnp.int32, (BLOCK, 1024), 0)
    cols = lax.broadcasted_iota(jnp.int32, (BLOCK, 1024), 1)
    least_m = jnp.where(first == 1, (3 - at) * BLOCK, 0)
    least_t = jnp.where(first == 1, (4 - at - core) * BLOCK, 0)
    bias_m = jnp.where((cols - 768 <= rows) & (cols >= least_m), 0.0, -1e30)
    bias_t = jnp.where((cols > rows) & (cols >= least_t), 0.0, -1e30)
    contract = (((1,), (1,)), ((), ()))
    for h in range(2):
        lanes = slice(h * HD, (h + 1) * HD)
        q = q_ref[at, :, lanes]
        km = km_ref[pl.ds(at + 1, 4), :, lanes].reshape(1024, HD)
        kt = kt_ref[pl.ds(at + core, 4), :, lanes].reshape(1024, HD)
        sm = lax.dot_general(q, km, contract, preferred_element_type=F32) + bias_m
        st = lax.dot_general(q, kt, contract, preferred_element_type=F32) + bias_t
        top = jnp.maximum(jnp.max(sm, axis=1, keepdims=True), jnp.max(st, axis=1, keepdims=True))
        pm = jnp.exp2(sm - top)
        pt = jnp.exp2(st - top)
        total = jnp.sum(pm, axis=1, keepdims=True) + jnp.sum(pt, axis=1, keepdims=True)
        vm = vm_ref[pl.ds(at + 1, 4), :, lanes].reshape(1024, HD)
        vt = vt_ref[pl.ds(at + core, 4), :, lanes].reshape(1024, HD)
        o = dot(pm.astype(BF), vm) + dot(pt.astype(BF), vt)
        o_ref[0, :, lanes] = (o / total).astype(BF)


def attention(place, offsets, q, km, kt, vm, vt):
    n = len(offsets)
    return pl.pallas_call(
        attention_kernel,
        grid=(n,),
        in_specs=[pl.BlockSpec(memory_space=pltpu.SMEM)] + in_vmem(5),
        out_specs=pl.BlockSpec((1, BLOCK, 256), lambda i: (i, 0, 0)),
        out_shape=jax.ShapeDtypeStruct((n, BLOCK, 256), BF),
        compiler_params=params(),
        cost_estimate=pl.CostEstimate(
            flops=n * 8 * BLOCK * 2048 * HD, bytes_accessed=5 << 20, transcendentals=n * 2 * BLOCK * 2048
        ),
    )(jnp.concatenate([place, jnp.array(offsets, jnp.int32)]), q, km, kt, vm, vt)


def collect_kernel(place_ref, a_ref, b_ref, c_ref, d_ref, o_ref):
    for dx, ref in enumerate((a_ref, b_ref, c_ref, d_ref)):
        at = lax.rem(place_ref[0] + 4 - dx, 4)
        o_ref[:, pl.ds(pl.multiple_of(at * 256, 256), 256)] = ref[0]


def collect(place, parts):
    return pl.pallas_call(
        collect_kernel,
        in_specs=[pl.BlockSpec(memory_space=pltpu.SMEM)] + in_vmem(4),
        out_specs=pl.BlockSpec(memory_space=pltpu.VMEM),
        out_shape=jax.ShapeDtypeStruct((BLOCK, 1024), BF),
        compiler_params=params(),
    )(place, *parts)


def on_device(
    audio_feats,
    res_conv,
    res_out,
    down_conv,
    stream_embed,
    turn_lengths,
    speaker_table,
    norm_gain,
    qkv_weight,
):
    tp = lax.axis_index("tp")
    x_at = lax.axis_index("x")
    core = lax.axis_index("c")
    row = lax.axis_index("yl") * 8 + lax.axis_index("z")
    audio = audio_feats[0]
    halo = lax.ppermute(audio[-8:], CTX, [(i, i + 1) for i in range(127)])
    latent = encoder(halo, audio, res_conv[0], res_out[0], down_conv[0])
    other = lax.ppermute(latent, "tp", SWAP)
    pieces = gather_latents(latent, other)

    m, lines = head_weights(stream_embed[0], speaker_table, norm_gain, qkv_weight)

    bounds = jnp.cumsum(turn_lengths, axis=1)
    start = ((row - 1 + jnp.arange(2)[:, None]) * 8 + 2 * jnp.arange(4)[None, :] + core) * BLOCK
    frames = (start[:, :, None] + jnp.arange(BLOCK)).reshape(8 * BLOCK)
    turn = jnp.sum((bounds[:, None, :] <= frames[None, :, None]).astype(jnp.int32), axis=2)
    active = (turn % 2 == 1).astype(F32)
    active_here = lax.dynamic_slice_in_dim(active, (4 + x_at) * BLOCK, BLOCK, 1)

    embed = stream_embed[0].reshape(CH, 2, D // 2)
    own = dot(latent, lax.dynamic_index_in_dim(embed, tp, 1, keepdims=False))
    give = dot(latent, lax.dynamic_index_in_dim(embed, 1 - tp, 1, keepdims=False)).astype(BF)
    got = lax.ppermute(give, "tp", SWAP)
    table = lax.dynamic_slice_in_dim(speaker_table, tp * (D // 2), D // 2, 1)
    x = own + got.astype(F32) + active_here[0][:, None] * table[0] + active_here[1][:, None] * table[1]
    embedded = x.astype(BF)
    square = jnp.sum(x * x, axis=1)
    square = square + lax.ppermute(square, "tp", SWAP)
    scale = lax.rsqrt(square * (1.0 / D) + 1e-05)
    scale_prev = lax.ppermute(scale, ("yl", "z"), [(i, i + 1) for i in range(15)])
    scales = jnp.broadcast_to(jnp.stack([scale_prev, scale])[None], (4, 2, BLOCK))
    scales = lax.all_to_all(scales, "x", 0, 0, tiled=True).transpose(1, 0, 2).reshape(8 * BLOCK)
    side = jnp.stack([active[0], active[1], scales] + [jnp.zeros_like(scales)] * 5, axis=1).reshape(8, BLOCK, 8)

    place = jnp.stack([x_at, lax.axis_index("yl")]).astype(jnp.int32)
    km, q = project(True, place, pieces, m, lines, side)
    kt = lax.ppermute(km, "c", SWAP)
    (vm,) = project(False, place, pieces, m, lines, side)
    vt = lax.ppermute(vm, "c", SWAP)

    place = jnp.stack([x_at, core, (row == 0).astype(jnp.int32)]).astype(jnp.int32)
    parts = [None] * 4
    for dx in (2, 1, 3, 0):
        part = attention(place, (dx,), q, km, kt, vm, vt)
        parts[dx] = lax.ppermute(part, "x", [(i, (i + dx) % 4) for i in range(4)]) if dx else part
    return embedded, collect(place, parts)


def solution(mesh):
    fine = Mesh(mesh.devices.reshape(2, 8, 4, 2, 2), CTX + ("tp",))
    placed = (
        P("tp", CTX, None),
        P("tp", None, None, None),
        P("tp", None, None),
        P("tp", None, None, None),
        P("tp", None, None),
        P(),
        P(),
        P(),
        P(None, CTX, "tp"),
    )
    return jax.shard_map(
        on_device,
        mesh=fine,
        in_specs=placed,
        out_specs=(P(CTX, "tp"), P(CTX, "tp")),
        check_vma=False,
    )
```

```python
import functools

import jax
import jax.numpy as jnp
from jax import lax
from jax.experimental import pallas as pl
from jax.experimental.pallas import tpu as pltpu
from jax.sharding import Mesh, PartitionSpec as P

HD = 128
BLOCK = 256
D = 4096
CH = 512
CTX = ("yl", "z", "x", "c")
SWAP = [(0, 1), (1, 0)]
BF = jnp.bfloat16
F32 = jnp.float32
LOG2E = 1.4426950408889634


def elu(v):
    return jnp.where(v > 0, v, jnp.exp(jnp.minimum(v, 0.0)) - 1.0)


def dot(a, b):
    return jnp.dot(a, b, preferred_element_type=F32)


def in_vmem(n):
    return [pl.BlockSpec(memory_space=pltpu.VMEM)] * n


def params(mib):
    return pltpu.CompilerParams(vmem_limit_bytes=mib * 1024 * 1024)


def encoder_kernel(halo_ref, audio_ref, taps_ref, back_ref, down_ref, out_ref, u_ref, e_ref):
    u_ref[0:8, :] = jnp.zeros((8, CH), F32)
    u_ref[8:16, :] = elu(halo_ref[...].astype(F32))
    u_ref[16:, :] = elu(audio_ref[...].astype(F32))
    rows = audio_ref.shape[0] + 8
    inner = dot(u_ref[2 : 2 + rows, :].astype(BF), taps_ref[0])
    inner += dot(u_ref[5 : 5 + rows, :].astype(BF), taps_ref[1])
    inner += dot(u_ref[8 : 8 + rows, :].astype(BF), taps_ref[2])
    hidden = elu(inner).astype(BF)
    branch = dot(hidden, back_ref[...])
    first = (halo_ref[...].astype(F32) + branch[0:8]).astype(BF)
    first = elu(first.astype(F32)).astype(BF).astype(F32)
    rest = (audio_ref[...].astype(F32) + branch[8:]).astype(BF)
    rest = elu(rest.astype(F32)).astype(BF).astype(F32)
    for j in range(CH // 128):
        e_ref[j, 0:8, :] = first[:, j * 128 : (j + 1) * 128]
        e_ref[j, 8:, :] = rest[:, j * 128 : (j + 1) * 128]
    acc = jnp.zeros((BLOCK, CH), F32)
    for k in range(4):
        e = [e_ref[j, pl.ds(6 + k, BLOCK, stride=2), :].astype(BF) for j in range(CH // 128)]
        acc += dot(jnp.concatenate(e, axis=1), down_ref[k])
    out_ref[...] = acc.astype(BF)


def encoder(halo, audio, taps, back, down):
    return pl.pallas_call(
        encoder_kernel,
        in_specs=in_vmem(5),
        out_specs=pl.BlockSpec(memory_space=pltpu.VMEM),
        out_shape=jax.ShapeDtypeStruct((BLOCK, CH), BF),
        scratch_shapes=[pltpu.VMEM((528, CH), F32), pltpu.VMEM((CH // 128, 520, 128), F32)],
        compiler_params=params(20),
        cost_estimate=pl.CostEstimate(flops=1100000000, bytes_accessed=4 << 20, transcendentals=600000),
    )(halo, audio, taps, back, down)


def swap(a, axis):
    return lax.ppermute(a, axis, SWAP)


def shift(a, by):
    return lax.ppermute(a, "x", [(i, (i + by) % 4) for i in range(4)])


def split_kernel(at_ref, w_ref, near_ref, far_ref, *outs):
    x = at_ref[3]
    for dx in range(4):
        lanes = pl.ds(pl.multiple_of(lax.rem(x + dx, 4) * 256, 256), 256)
        outs[dx][...] = w_ref[:, :, lanes]
    outs[4][0] = near_ref[...]
    outs[4][1] = far_ref[...]


def split(at, w, embed):
    whole = lambda shape: pl.BlockSpec(shape, lambda i, at: (0,) * len(shape))
    return pl.pallas_call(
        split_kernel,
        grid_spec=pltpu.PrefetchScalarGridSpec(
            num_scalar_prefetch=1,
            grid=(1,),
            in_specs=[
                whole((3, 32, 1024)),
                pl.BlockSpec((128, 256), lambda i, at: (at[2], at[0])),
                pl.BlockSpec((128, 256), lambda i, at: (at[2], at[1])),
            ],
            out_specs=[whole((3, 32, 256))] * 4 + [whole((2, 128, 256))],
        ),
        out_shape=[jax.ShapeDtypeStruct((3, 32, 256), BF)] * 4 + [jax.ShapeDtypeStruct((2, 128, 256), BF)],
    )(at, w, embed, embed)


def partial_kernel(at_ref, w00, w01, w10, w11, mine_ref, rest_ref, g0, g1, t0, t1, out_ref, w_ref):
    x, core = at_ref[3], at_ref[4]
    for y, pair in enumerate(((w00, w01), (w10, w11))):
        for c, ref in enumerate(pair):
            for dx in range(4):
                row = lax.rem(x + 4 - dx, 4) * 64 + (core ^ c) * 32
                for j in range(3):
                    w_ref[y, pl.ds(pl.multiple_of(row, 32), 32), j * 256 : (j + 1) * 256] = ref[dx, j]
    part = None
    line = None
    for y, (gain_ref, table_ref) in enumerate(((g0, t0), (g1, t1))):
        w = w_ref[y]
        gain = gain_ref[...]
        embed = jnp.concatenate([mine_ref[y], rest_ref[y]], axis=0).astype(F32) * gain
        table = jnp.concatenate([table_ref[...], jnp.zeros((6, 256), F32)], axis=0) * gain
        high = table.astype(BF)
        low = (table - high.astype(F32)).astype(BF)
        a = dot(embed.astype(BF), w)
        b = dot(high, w) + dot(low, w)
        part = a if part is None else part + a
        line = b if line is None else line + b
    top = line.astype(BF).astype(F32)
    rem = line - top
    rows = [v[s : s + 1, k * 128 : (k + 1) * 128] for v in (top, rem) for s in range(2) for k in range(6)]
    tail = jnp.concatenate(rows + [jnp.zeros((8, 128), F32)], axis=0).astype(BF)
    for i in range(8):
        out_ref[i, :, 0:768] = part[i * 32 : (i + 1) * 32].astype(BF)
        out_ref[i, :, 768:896] = tail


def partial_weights(at, ws, mine, rest, gain, table):
    whole = lambda shape: pl.BlockSpec(shape, lambda i, at: (0,) * len(shape))
    here = lambda rows, k: pl.BlockSpec((rows, 256), lambda i, at: (0, at[k]))
    return pl.pallas_call(
        partial_kernel,
        grid_spec=pltpu.PrefetchScalarGridSpec(
            num_scalar_prefetch=1,
            grid=(1,),
            in_specs=[whole((4, 3, 32, 256))] * 4
            + [whole((2, 128, 256))] * 2
            + [here(1, 0), here(1, 1), here(2, 0), here(2, 1)],
            out_specs=whole((8, 32, 896)),
            scratch_shapes=[pltpu.VMEM((2, 256, 768), BF)],
        ),
        out_shape=jax.ShapeDtypeStruct((8, 32, 896), BF),
        compiler_params=params(16),
        cost_estimate=pl.CostEstimate(flops=210000000, bytes_accessed=2 << 20, transcendentals=0),
    )(at, *ws, mine, rest, gain, gain, table, table)


def sum_kernel(p_ref, m_ref, line_ref):
    total = jnp.sum(p_ref[...].astype(F32), axis=0)
    m = total[:, :768].astype(BF)
    for i in range(8):
        m_ref[i] = m
    both = total[0:12, 768:] + total[12:24, 768:]
    line_ref[...] = jnp.zeros((8, 768), F32)
    for s in range(2):
        for k in range(6):
            line_ref[s : s + 1, k * 128 : (k + 1) * 128] = both[s * 6 + k : s * 6 + k + 1]


def sum_weights(packed):
    return pl.pallas_call(
        sum_kernel,
        in_specs=in_vmem(1),
        out_specs=in_vmem(2),
        out_shape=[jax.ShapeDtypeStruct((8, 32, 768), BF), jax.ShapeDtypeStruct((8, 768), F32)],
        compiler_params=params(8),
    )(packed)


def give_kernel(at_ref, latent_ref, embed_ref, *refs):
    refs[-1][...] = dot(latent_ref[...], embed_ref[...]).astype(BF)


def give_term(at, latent, embed, after):
    return pl.pallas_call(
        give_kernel,
        grid_spec=pltpu.PrefetchScalarGridSpec(
            num_scalar_prefetch=1,
            grid=(2,),
            in_specs=[
                pl.BlockSpec((BLOCK, CH), lambda i, at: (0, 0)),
                pl.BlockSpec((CH, 1024), lambda i, at: (0, (1 - at[5]) * 2 + i)),
            ]
            + [pl.BlockSpec(memory_space=pl.ANY)] * len(after),
            out_specs=pl.BlockSpec((BLOCK, 1024), lambda i, at: (0, i)),
        ),
        out_shape=jax.ShapeDtypeStruct((BLOCK, D // 2), BF),
        compiler_params=params(16),
        cost_estimate=pl.CostEstimate(flops=540000000, bytes_accessed=3 << 20, transcendentals=0),
    )(at, latent, embed, *after)


def embed_kernel(at_ref, latent_ref, embed_ref, got_ref, active_ref, table_ref, out_ref, square_ref):
    act = active_ref[:, pl.ds(at_ref[3] + 4, 1), :].reshape(2, BLOCK)
    cols = jnp.concatenate([act, jnp.zeros((6, BLOCK), F32)], axis=0).T
    x = dot(latent_ref[...], embed_ref[...]) + got_ref[...].astype(F32)
    x = x + cols[:, 0:1] * table_ref[0:1] + cols[:, 1:2] * table_ref[1:2]
    out_ref[...] = x.astype(BF)
    square = jnp.sum(x * x, axis=1, keepdims=True)
    square = jnp.broadcast_to(square, (BLOCK, 128)).T[0:8]

    @pl.when(pl.program_id(0) == 0)
    def _():
        square_ref[...] = square

    @pl.when(pl.program_id(0) != 0)
    def _():
        square_ref[...] += square


def embed_rows(at, latent, embed, got, active, table):
    mine = lambda rows: pl.BlockSpec((rows, 1024), lambda i, at: (0, at[5] * 2 + i))
    tile = pl.BlockSpec((BLOCK, 1024), lambda i, at: (0, i))
    return pl.pallas_call(
        embed_kernel,
        grid_spec=pltpu.PrefetchScalarGridSpec(
            num_scalar_prefetch=1,
            grid=(2,),
            in_specs=[
                pl.BlockSpec((BLOCK, CH), lambda i, at: (0, 0)),
                mine(CH),
                tile,
                pl.BlockSpec((2, 8, BLOCK), lambda i, at: (0, 0, 0)),
                mine(2),
            ],
            out_specs=[tile, pl.BlockSpec((8, BLOCK), lambda i, at: (0, 0))],
        ),
        out_shape=[jax.ShapeDtypeStruct((BLOCK, D // 2), BF), jax.ShapeDtypeStruct((8, BLOCK), F32)],
        compiler_params=params(20),
        cost_estimate=pl.CostEstimate(flops=540000000, bytes_accessed=5 << 20, transcendentals=0),
    )(at, latent, embed, got, active, table)


def project_kernel(with_q, at_ref, *refs):
    (a, al, ar, af, b, bl, br, bf, m00, m01, m10, m11, line_ref, active_ref, s0, s1, s2, s3) = refs[:18]
    outs, m_ref = refs[18:-1], refs[-1]
    x, core, yl = at_ref[3], at_ref[4], at_ref[6]
    lanes = slice(0, 512) if with_q else slice(512, 768)
    for y, pair in enumerate(((m00, m01), (m10, m11))):
        for c, ref in enumerate(pair):
            row = ((yl ^ y) * 2 + (core ^ c)) * 128
            for s in range(2):
                m_ref[pl.ds(pl.multiple_of(s * 512 + row, 128), 128), :] = ref[s * 128 : (s + 1) * 128, lanes]
    own = (a, ar, af, al)
    prev = (b, br, bf, bl)
    scales = (s0, s1, s2, s3)
    jobs = [(0, outs[1], 0), (1, outs[0], 1)] if with_q else [(2, outs[0], 1)]
    for r, blocks in ((1, own), (0, prev)):
        for dx in range(4):
            at = lax.rem(x + dx, 4)
            m = 4 * r + at
            act = active_ref[:, pl.ds(m, 1), :].reshape(2, BLOCK)
            side = jnp.concatenate([act, scales[dx][r : r + 1, :], jnp.zeros((5, BLOCK), F32)], axis=0).T
            rows = blocks[dx]
            for j, out, both in jobs:
                if not both and r == 0:
                    continue
                at_j = j * 256 - lanes.start
                line = line_ref[:, j * 256 : (j + 1) * 256]
                acc = dot(rows[0], m_ref[0:512, at_j : at_j + 256]) + dot(rows[1], m_ref[512:1024, at_j : at_j + 256])
                acc = acc + side[:, 0:1] * line[0:1] + side[:, 1:2] * line[1:2]
                acc = acc * (side[:, 2:3] * (HD**-0.5 * LOG2E if j == 0 else 1.0))
                out[m if both else at] = acc.astype(BF)


def project(with_q, at, pieces, ms, lines, active, scales):
    shapes = [jax.ShapeDtypeStruct((8, BLOCK, 256), BF)]
    if with_q:
        shapes.append(jax.ShapeDtypeStruct((4, BLOCK, 256), BF))
    return pl.pallas_call(
        functools.partial(project_kernel, with_q),
        in_specs=[pl.BlockSpec(memory_space=pltpu.SMEM)] + in_vmem(18),
        out_specs=in_vmem(len(shapes)),
        out_shape=shapes,
        scratch_shapes=[pltpu.VMEM((1024, 512 if with_q else 256), BF)],
        compiler_params=params(20),
        cost_estimate=pl.CostEstimate(flops=1600000000, bytes_accessed=6 << 20, transcendentals=0),
    )(at, *pieces, *ms, lines, active, *scales)


def attention_kernel(place_ref, q_ref, km_ref, kt_ref, vm_ref, vt_ref, o_ref):
    at = lax.rem(place_ref[0] + place_ref[3 + pl.program_id(0)], 4)
    core = place_ref[1]
    first = place_ref[2]
    rows = lax.broadcasted_iota(jnp.int32, (BLOCK, 1024), 0)
    cols = lax.broadcasted_iota(jnp.int32, (BLOCK, 1024), 1)
    least_m = jnp.where(first == 1, (3 - at) * BLOCK, 0)
    least_t = jnp.where(first == 1, (4 - at - core) * BLOCK, 0)
    bias_m = jnp.where((cols - 768 <= rows) & (cols >= least_m), 0.0, -1e30)
    bias_t = jnp.where((cols > rows) & (cols >= least_t), 0.0, -1e30)
    contract = (((1,), (1,)), ((), ()))
    for h in range(2):
        lanes = slice(h * HD, (h + 1) * HD)
        q = q_ref[at, :, lanes]
        km = km_ref[pl.ds(at + 1, 4), :, lanes].reshape(1024, HD)
        kt = kt_ref[pl.ds(at + core, 4), :, lanes].reshape(1024, HD)
        sm = lax.dot_general(q, km, contract, preferred_element_type=F32) + bias_m
        st = lax.dot_general(q, kt, contract, preferred_element_type=F32) + bias_t
        top = jnp.maximum(jnp.max(sm, axis=1, keepdims=True), jnp.max(st, axis=1, keepdims=True))
        pm = jnp.exp2(sm - top)
        pt = jnp.exp2(st - top)
        total = jnp.sum(pm, axis=1, keepdims=True) + jnp.sum(pt, axis=1, keepdims=True)
        vm = vm_ref[pl.ds(at + 1, 4), :, lanes].reshape(1024, HD)
        vt = vt_ref[pl.ds(at + core, 4), :, lanes].reshape(1024, HD)
        o = dot(pm.astype(BF), vm) + dot(pt.astype(BF), vt)
        o_ref[0, :, lanes] = (o / total).astype(BF)


def attention(place, offsets, q, km, kt, vm, vt):
    n = len(offsets)
    return pl.pallas_call(
        attention_kernel,
        grid=(n,),
        in_specs=[pl.BlockSpec(memory_space=pltpu.SMEM)] + in_vmem(5),
        out_specs=pl.BlockSpec((1, BLOCK, 256), lambda i: (i, 0, 0)),
        out_shape=jax.ShapeDtypeStruct((n, BLOCK, 256), BF),
        compiler_params=params(20),
        cost_estimate=pl.CostEstimate(
            flops=n * 8 * BLOCK * 2048 * HD, bytes_accessed=5 << 20, transcendentals=n * 2 * BLOCK * 2048
        ),
    )(jnp.concatenate([place, jnp.array(offsets, jnp.int32)]), q, km, kt, vm, vt)


def collect_kernel(place_ref, a_ref, b_ref, c_ref, d_ref, o_ref):
    for dx, ref in enumerate((a_ref, b_ref, c_ref, d_ref)):
        at = lax.rem(place_ref[0] + 4 - dx, 4)
        o_ref[:, pl.ds(pl.multiple_of(at * 256, 256), 256)] = ref[0]


def collect(place, parts):
    return pl.pallas_call(
        collect_kernel,
        in_specs=[pl.BlockSpec(memory_space=pltpu.SMEM)] + in_vmem(4),
        out_specs=pl.BlockSpec(memory_space=pltpu.VMEM),
        out_shape=jax.ShapeDtypeStruct((BLOCK, 1024), BF),
        compiler_params=params(20),
    )(place, *parts)


def on_device(
    audio_feats,
    res_conv,
    res_out,
    down_conv,
    stream_embed,
    turn_lengths,
    speaker_table,
    norm_gain,
    qkv_weight,
):
    tp = lax.axis_index("tp")
    x_at = lax.axis_index("x")
    core = lax.axis_index("c")
    yl = lax.axis_index("yl")
    z = lax.axis_index("z")
    row = yl * 8 + z
    at = jnp.stack([yl * 8 + z, (1 - yl) * 8 + z, yl * 2 + core, x_at, core, tp, yl]).astype(jnp.int32)
    behind = [(i, i + 1) for i in range(15)]

    audio = audio_feats[0]
    halo = lax.ppermute(audio[-8:], CTX, [(i, i + 1) for i in range(127)])
    embed = stream_embed[0]
    *chunks, mine = split(at, qkv_weight, embed)
    w00 = jnp.stack([chunks[0]] + [shift(chunks[dx], dx) for dx in (1, 2, 3)])
    rest = swap(mine, "tp")
    w10 = swap(w00, "yl")
    w01 = swap(w00, "c")
    w11 = swap(w10, "c")

    latent = encoder(halo, audio, res_conv[0], res_out[0], down_conv[0])
    other = swap(latent, "tp")
    prev = lax.ppermute(latent, ("yl", "z"), behind)
    a = jnp.stack([latent, other])
    al, ar = shift(a, 1), shift(a, 3)
    b = jnp.stack([prev, lax.ppermute(other, ("yl", "z"), behind)])
    bl, br = shift(b, 1), shift(b, 3)
    pieces = (a, al, ar, shift(al, 1), b, bl, br, shift(br, 3))

    packed = partial_weights(at, (w00, w01, w10, w11), mine, rest, norm_gain[None], speaker_table)
    packed = lax.all_to_all(packed, "z", 0, 0, tiled=True)
    m, lines = sum_weights(packed)
    m00 = lax.all_to_all(m, "z", 0, 0, tiled=True).reshape(256, 768)
    m10 = swap(m00, "yl")
    m01 = swap(m00, "c")
    m11 = swap(m10, "c")

    bounds = jnp.cumsum(turn_lengths, axis=1)
    start = ((row - 1 + jnp.arange(2)[:, None]) * 8 + 2 * jnp.arange(4)[None, :] + core) * BLOCK
    frames = start.reshape(8, 1) + jnp.arange(BLOCK)
    turn = jnp.sum((bounds[:, :, None, None] <= frames[None, None]).astype(jnp.int32), axis=1)
    active = (turn % 2 == 1).astype(F32)

    got = swap(give_term(at, latent, embed, (other, w11)), "tp")
    embedded, square = embed_rows(at, latent, embed, got, active, speaker_table)
    square = square + swap(square, "tp")
    scale = lax.rsqrt(square[0:1] * (1.0 / D) + 1e-05)
    scale = jnp.concatenate([lax.ppermute(scale, ("yl", "z"), behind), scale])
    scales = [scale] + [shift(scale, 4 - dx) for dx in (1, 2, 3)]

    ms = (m00, m01, m10, m11)
    km, q = project(True, at, pieces, ms, lines, active, scales)
    kt = swap(km, "c")
    (vm,) = project(False, at, pieces, ms, lines, active, scales)
    vt = swap(vm, "c")

    place = jnp.stack([x_at, core, (row == 0).astype(jnp.int32)]).astype(jnp.int32)
    parts = [None] * 4
    for dx in (2, 1, 3, 0):
        part = attention(place, (dx,), q, km, kt, vm, vt)
        parts[dx] = shift(part, dx) if dx else part
    return embedded, collect(place, parts)


def solution(mesh):
    fine = Mesh(mesh.devices.reshape(2, 8, 4, 2, 2), CTX + ("tp",))
    placed = (
        P("tp", CTX, None),
        P("tp", None, None, None),
        P("tp", None, None),
        P("tp", None, None, None),
        P("tp", None, None),
        P(),
        P(),
        P(),
        P(None, CTX, "tp"),
    )
    return jax.shard_map(
        on_device,
        mesh=fine,
        in_specs=placed,
        out_specs=(P(CTX, "tp"), P(CTX, "tp")),
        check_vma=False,
    )
```

```python
import functools

import jax
import jax.numpy as jnp
from jax import lax
from jax.experimental import pallas as pl
from jax.experimental.pallas import tpu as pltpu
from jax.sharding import Mesh, PartitionSpec as P

HD = 128
BLOCK = 256
D = 4096
CH = 512
CTX = ("yl", "z", "x", "c")
SWAP = [(0, 1), (1, 0)]
BF = jnp.bfloat16
F32 = jnp.float32
LOG2E = 1.4426950408889634


def elu(v):
    return jnp.where(v > 0, v, jnp.exp(jnp.minimum(v, 0.0)) - 1.0)


def dot(a, b):
    return jnp.dot(a, b, preferred_element_type=F32)


def in_vmem(n):
    return [pl.BlockSpec(memory_space=pltpu.VMEM)] * n


def params(mib):
    return pltpu.CompilerParams(vmem_limit_bytes=mib * 1024 * 1024)


def encoder_kernel(halo_ref, audio_ref, taps_ref, back_ref, down_ref, out_ref, u_ref, e_ref):
    u_ref[0:8, :] = jnp.zeros((8, CH), F32)
    u_ref[8:16, :] = elu(halo_ref[...].astype(F32))
    u_ref[16:, :] = elu(audio_ref[...].astype(F32))
    rows = audio_ref.shape[0] + 8
    inner = dot(u_ref[2 : 2 + rows, :].astype(BF), taps_ref[0])
    inner += dot(u_ref[5 : 5 + rows, :].astype(BF), taps_ref[1])
    inner += dot(u_ref[8 : 8 + rows, :].astype(BF), taps_ref[2])
    hidden = elu(inner).astype(BF)
    branch = dot(hidden, back_ref[...])
    first = (halo_ref[...].astype(F32) + branch[0:8]).astype(BF)
    first = elu(first.astype(F32)).astype(BF).astype(F32)
    rest = (audio_ref[...].astype(F32) + branch[8:]).astype(BF)
    rest = elu(rest.astype(F32)).astype(BF).astype(F32)
    for j in range(CH // 128):
        e_ref[j, 0:8, :] = first[:, j * 128 : (j + 1) * 128]
        e_ref[j, 8:, :] = rest[:, j * 128 : (j + 1) * 128]
    acc = jnp.zeros((BLOCK, CH), F32)
    for k in range(4):
        e = [e_ref[j, pl.ds(6 + k, BLOCK, stride=2), :].astype(BF) for j in range(CH // 128)]
        acc += dot(jnp.concatenate(e, axis=1), down_ref[k])
    out_ref[...] = acc.astype(BF)


def encoder(halo, audio, taps, back, down):
    return pl.pallas_call(
        encoder_kernel,
        in_specs=in_vmem(5),
        out_specs=pl.BlockSpec(memory_space=pltpu.VMEM),
        out_shape=jax.ShapeDtypeStruct((BLOCK, CH), BF),
        scratch_shapes=[pltpu.VMEM((528, CH), F32), pltpu.VMEM((CH // 128, 520, 128), F32)],
        compiler_params=params(20),
        cost_estimate=pl.CostEstimate(flops=1100000000, bytes_accessed=4 << 20, transcendentals=600000),
    )(halo, audio, taps, back, down)


def swap(a, axis):
    return lax.ppermute(a, axis, SWAP)


def shift(a, by):
    return lax.ppermute(a, "x", [(i, (i + by) % 4) for i in range(4)])


def split_kernel(at_ref, w_ref, near_ref, far_ref, *outs):
    x = at_ref[3]
    for dx in range(4):
        lanes = pl.ds(pl.multiple_of(lax.rem(x + dx, 4) * 256, 256), 256)
        outs[dx][...] = w_ref[:, :, lanes]
    outs[4][0] = near_ref[...]
    outs[4][1] = far_ref[...]


def split(at, w, embed):
    whole = lambda shape: pl.BlockSpec(shape, lambda i, at: (0,) * len(shape))
    return pl.pallas_call(
        split_kernel,
        grid_spec=pltpu.PrefetchScalarGridSpec(
            num_scalar_prefetch=1,
            grid=(1,),
            in_specs=[
                whole((3, 32, 1024)),
                pl.BlockSpec((128, 256), lambda i, at: (at[2], at[0])),
                pl.BlockSpec((128, 256), lambda i, at: (at[2], at[1])),
            ],
            out_specs=[whole((3, 32, 256))] * 4 + [whole((2, 128, 256))],
        ),
        out_shape=[jax.ShapeDtypeStruct((3, 32, 256), BF)] * 4 + [jax.ShapeDtypeStruct((2, 128, 256), BF)],
    )(at, w, embed, embed)


def unused(after):
    return [pl.BlockSpec(memory_space=pl.ANY)] * len(after)


def stack_kernel(n, *refs):
    for i in range(n):
        refs[-1][i] = refs[i][...]


def stack(parts, after=()):
    return pl.pallas_call(
        functools.partial(stack_kernel, len(parts)),
        in_specs=in_vmem(len(parts)) + unused(after),
        out_specs=pl.BlockSpec(memory_space=pltpu.VMEM),
        out_shape=jax.ShapeDtypeStruct((len(parts),) + parts[0].shape, parts[0].dtype),
        compiler_params=params(4),
    )(*parts, *after)


def partial_kernel(at_ref, w00, w01, w10, w11, mine_ref, rest_ref, g0, g1, t0, t1, *refs):
    out_ref, w_ref = refs[-2:]
    x, core = at_ref[3], at_ref[4]
    for y, pair in enumerate(((w00, w01), (w10, w11))):
        for c, ref in enumerate(pair):
            for dx in range(4):
                row = lax.rem(x + 4 - dx, 4) * 64 + (core ^ c) * 32
                for j in range(3):
                    w_ref[y, pl.ds(pl.multiple_of(row, 32), 32), j * 256 : (j + 1) * 256] = ref[dx, j]
    part = None
    line = None
    for y, (gain_ref, table_ref) in enumerate(((g0, t0), (g1, t1))):
        w = w_ref[y]
        gain = gain_ref[...]
        embed = jnp.concatenate([mine_ref[y], rest_ref[y]], axis=0).astype(F32) * gain
        table = jnp.concatenate([table_ref[...], jnp.zeros((6, 256), F32)], axis=0) * gain
        high = table.astype(BF)
        low = (table - high.astype(F32)).astype(BF)
        a = dot(embed.astype(BF), w)
        b = dot(high, w) + dot(low, w)
        part = a if part is None else part + a
        line = b if line is None else line + b
    top = line.astype(BF).astype(F32)
    rem = line - top
    rows = [v[s : s + 1, k * 128 : (k + 1) * 128] for v in (top, rem) for s in range(2) for k in range(6)]
    tail = jnp.concatenate(rows + [jnp.zeros((8, 128), F32)], axis=0).astype(BF)
    for i in range(8):
        out_ref[i, :, 0:768] = part[i * 32 : (i + 1) * 32].astype(BF)
        out_ref[i, :, 768:896] = tail


def partial_weights(at, ws, mine, rest, gain, table, after):
    whole = lambda shape: pl.BlockSpec(shape, lambda i, at: (0,) * len(shape))
    here = lambda rows, k: pl.BlockSpec((rows, 256), lambda i, at: (0, at[k]))
    return pl.pallas_call(
        partial_kernel,
        grid_spec=pltpu.PrefetchScalarGridSpec(
            num_scalar_prefetch=1,
            grid=(1,),
            in_specs=[whole((4, 3, 32, 256))] * 4
            + [whole((2, 128, 256))] * 2
            + [here(1, 0), here(1, 1), here(2, 0), here(2, 1)]
            + unused(after),
            out_specs=whole((8, 32, 896)),
            scratch_shapes=[pltpu.VMEM((2, 256, 768), BF)],
        ),
        out_shape=jax.ShapeDtypeStruct((8, 32, 896), BF),
        compiler_params=params(16),
        cost_estimate=pl.CostEstimate(flops=210000000, bytes_accessed=2 << 20, transcendentals=0),
    )(at, *ws, mine, rest, gain, gain, table, table, *after)


def sum_kernel(p_ref, *refs):
    m_ref, line_ref = refs[-2:]
    total = jnp.sum(p_ref[...].astype(F32), axis=0)
    m = total[:, :768].astype(BF)
    for i in range(8):
        m_ref[i] = m
    both = total[0:12, 768:] + total[12:24, 768:]
    line_ref[...] = jnp.zeros((8, 768), F32)
    for s in range(2):
        for k in range(6):
            line_ref[s : s + 1, k * 128 : (k + 1) * 128] = both[s * 6 + k : s * 6 + k + 1]


def sum_weights(packed, after):
    return pl.pallas_call(
        sum_kernel,
        in_specs=in_vmem(1) + unused(after),
        out_specs=in_vmem(2),
        out_shape=[jax.ShapeDtypeStruct((8, 32, 768), BF), jax.ShapeDtypeStruct((8, 768), F32)],
        compiler_params=params(8),
    )(packed, *after)


def give_kernel(at_ref, latent_ref, embed_ref, *refs):
    refs[-1][...] = dot(latent_ref[...], embed_ref[...]).astype(BF)


def give_term(at, latent, embed, after):
    return pl.pallas_call(
        give_kernel,
        grid_spec=pltpu.PrefetchScalarGridSpec(
            num_scalar_prefetch=1,
            grid=(2,),
            in_specs=[
                pl.BlockSpec((BLOCK, CH), lambda i, at: (0, 0)),
                pl.BlockSpec((CH, 1024), lambda i, at: (0, (1 - at[5]) * 2 + i)),
            ]
            + unused(after),
            out_specs=pl.BlockSpec((BLOCK, 1024), lambda i, at: (0, i)),
        ),
        out_shape=jax.ShapeDtypeStruct((BLOCK, D // 2), BF),
        compiler_params=params(16),
        cost_estimate=pl.CostEstimate(flops=540000000, bytes_accessed=3 << 20, transcendentals=0),
    )(at, latent, embed, *after)


def embed_kernel(at_ref, latent_ref, embed_ref, got_ref, active_ref, table_ref, out_ref, square_ref):
    act = active_ref[:, pl.ds(at_ref[3] + 4, 1), :].reshape(2, BLOCK)
    cols = jnp.concatenate([act, jnp.zeros((6, BLOCK), F32)], axis=0).T
    x = dot(latent_ref[...], embed_ref[...]) + got_ref[...].astype(F32)
    x = x + cols[:, 0:1] * table_ref[0:1] + cols[:, 1:2] * table_ref[1:2]
    out_ref[...] = x.astype(BF)
    square = jnp.sum(x * x, axis=1, keepdims=True)
    square = jnp.broadcast_to(square, (BLOCK, 128)).T[0:8]

    @pl.when(pl.program_id(0) == 0)
    def _():
        square_ref[...] = square

    @pl.when(pl.program_id(0) != 0)
    def _():
        square_ref[...] += square


def embed_rows(at, latent, embed, got, active, table):
    mine = lambda rows: pl.BlockSpec((rows, 1024), lambda i, at: (0, at[5] * 2 + i))
    tile = pl.BlockSpec((BLOCK, 1024), lambda i, at: (0, i))
    return pl.pallas_call(
        embed_kernel,
        grid_spec=pltpu.PrefetchScalarGridSpec(
            num_scalar_prefetch=1,
            grid=(2,),
            in_specs=[
                pl.BlockSpec((BLOCK, CH), lambda i, at: (0, 0)),
                mine(CH),
                tile,
                pl.BlockSpec((2, 8, BLOCK), lambda i, at: (0, 0, 0)),
                mine(2),
            ],
            out_specs=[tile, pl.BlockSpec((8, BLOCK), lambda i, at: (0, 0))],
        ),
        out_shape=[jax.ShapeDtypeStruct((BLOCK, D // 2), BF), jax.ShapeDtypeStruct((8, BLOCK), F32)],
        compiler_params=params(20),
        cost_estimate=pl.CostEstimate(flops=540000000, bytes_accessed=5 << 20, transcendentals=0),
    )(at, latent, embed, got, active, table)


def project_rows(row, blocks, m_ref, line_ref, active_ref, scales, at_ref, kv_ref, q_ref):
    x = at_ref[3]
    cols = slice(0, 768) if q_ref is not None else slice(256, 768)
    w0, w1 = m_ref[0:512, cols], m_ref[512:1024, cols]
    line = line_ref[:, cols]
    for dx in range(4):
        at = lax.rem(x + dx, 4)
        act = active_ref[:, pl.ds(4 * row + at, 1), :].reshape(2, BLOCK)
        side = jnp.concatenate([act, scales[dx][row : row + 1, :], jnp.zeros((5, BLOCK), F32)], axis=0).T
        acc = dot(blocks[dx][0], w0) + dot(blocks[dx][1], w1)
        acc = (acc + side[:, 0:1] * line[0:1] + side[:, 1:2] * line[1:2]) * side[:, 2:3]
        kv_ref[at] = acc[:, -512:].astype(BF)
        if q_ref is not None:
            q_ref[at] = (acc[:, :256] * (HD**-0.5 * LOG2E)).astype(BF)


def project_own_kernel(at_ref, a, al, ar, af, m00, m01, m10, m11, line_ref, active_ref, s0, s1, s2, s3, kv_ref, q_ref, m_ref):
    core, yl = at_ref[4], at_ref[6]
    for y, pair in enumerate(((m00, m01), (m10, m11))):
        for c, ref in enumerate(pair):
            row = ((yl ^ y) * 2 + (core ^ c)) * 128
            for s in range(2):
                m_ref[pl.ds(pl.multiple_of(s * 512 + row, 128), 128), :] = ref[s * 128 : (s + 1) * 128, :]
    project_rows(1, (a, ar, af, al), m_ref, line_ref, active_ref, (s0, s1, s2, s3), at_ref, kv_ref, q_ref)


def project_prev_kernel(at_ref, b, bl, br, bf, m_ref, line_ref, active_ref, s0, s1, s2, s3, kv_ref):
    project_rows(0, (b, br, bf, bl), m_ref, line_ref, active_ref, (s0, s1, s2, s3), at_ref, kv_ref, None)


def project(kernel, outs, *args):
    return pl.pallas_call(
        kernel,
        in_specs=[pl.BlockSpec(memory_space=pltpu.SMEM)] + in_vmem(len(args) - 1),
        out_specs=in_vmem(len(outs)),
        out_shape=[jax.ShapeDtypeStruct(o, BF) for o in outs],
        compiler_params=params(16),
        cost_estimate=pl.CostEstimate(flops=1600000000, bytes_accessed=6 << 20, transcendentals=0),
    )(*args)


def attention_kernel(place_ref, q_ref, om_ref, ot_ref, pm_ref, pt_ref, o_ref):
    at = lax.rem(place_ref[0] + place_ref[3], 4)
    core = place_ref[1]
    first = place_ref[2]
    rows = lax.broadcasted_iota(jnp.int32, (BLOCK, BLOCK), 0)
    cols = lax.broadcasted_iota(jnp.int32, (BLOCK, BLOCK), 1)
    blocks = []
    for own_ref, prev_ref, begin in ((om_ref, pm_ref, at + 1), (ot_ref, pt_ref, at + core)):
        for j in range(4):
            m = begin + j
            i = lax.rem(m, 4)
            blocks.append((jnp.where(m >= 4, own_ref[i], prev_ref[i]), jnp.where((m < 4) & (first == 1), 1e30, 0.0)))
    contract = (((1,), (1,)), ((), ()))
    for h in range(2):
        q = q_ref[at, :, h * HD : (h + 1) * HD]
        scores = []
        top = None
        for n, (kv, penalty) in enumerate(blocks):
            s = lax.dot_general(q, kv[:, h * HD : (h + 1) * HD], contract, preferred_element_type=F32)
            if n == 3:
                s = jnp.where(cols <= rows, s, -1e30)
            if n == 4:
                s = jnp.where(cols > rows, s, -1e30)
            most = jnp.max(s, axis=1, keepdims=True) - penalty
            top = most if top is None else jnp.maximum(top, most)
            scores.append(s)
        total = jnp.zeros((BLOCK, 1), F32)
        o = jnp.zeros((BLOCK, HD), F32)
        for s, (kv, penalty) in zip(scores, blocks):
            p = jnp.exp2(s - (top + penalty))
            total += jnp.sum(p, axis=1, keepdims=True)
            o += dot(p.astype(BF), kv[:, 256 + h * HD : 256 + (h + 1) * HD])
        o_ref[0, :, h * HD : (h + 1) * HD] = (o / total).astype(BF)


def attention(place, dx, *args):
    return pl.pallas_call(
        attention_kernel,
        in_specs=[pl.BlockSpec(memory_space=pltpu.SMEM)] + in_vmem(5),
        out_specs=pl.BlockSpec(memory_space=pltpu.VMEM),
        out_shape=jax.ShapeDtypeStruct((1, BLOCK, 256), BF),
        compiler_params=params(16),
        cost_estimate=pl.CostEstimate(flops=8 * BLOCK * 2048 * HD, bytes_accessed=5 << 20, transcendentals=2 * BLOCK * 2048),
    )(jnp.concatenate([place, jnp.array([dx], jnp.int32)]), *args)


def collect_kernel(place_ref, a_ref, b_ref, c_ref, d_ref, o_ref):
    for dx, ref in enumerate((a_ref, b_ref, c_ref, d_ref)):
        at = lax.rem(place_ref[0] + 4 - dx, 4)
        o_ref[:, pl.ds(pl.multiple_of(at * 256, 256), 256)] = ref[0]


def collect(place, parts):
    return pl.pallas_call(
        collect_kernel,
        in_specs=[pl.BlockSpec(memory_space=pltpu.SMEM)] + in_vmem(4),
        out_specs=pl.BlockSpec(memory_space=pltpu.VMEM),
        out_shape=jax.ShapeDtypeStruct((BLOCK, 1024), BF),
        compiler_params=params(20),
    )(place, *parts)


def on_device(
    audio_feats,
    res_conv,
    res_out,
    down_conv,
    stream_embed,
    turn_lengths,
    speaker_table,
    norm_gain,
    qkv_weight,
):
    tp = lax.axis_index("tp")
    x_at = lax.axis_index("x")
    core = lax.axis_index("c")
    yl = lax.axis_index("yl")
    z = lax.axis_index("z")
    row = yl * 8 + z
    at = jnp.stack([yl * 8 + z, (1 - yl) * 8 + z, yl * 2 + core, x_at, core, tp, yl]).astype(jnp.int32)
    behind = [(i, i + 1) for i in range(15)]

    audio = audio_feats[0]
    halo = lax.ppermute(audio[-8:], CTX, [(i, i + 1) for i in range(127)])
    embed = stream_embed[0]
    *chunks, mine = split(at, qkv_weight, embed)
    arrived = [shift(chunks[dx], dx) for dx in (1, 2, 3)]
    rest = swap(mine, "tp")

    latent = encoder(halo, audio, res_conv[0], res_out[0], down_conv[0])
    other = swap(latent, "tp")
    a = stack([latent, other])
    al, ar = shift(a, 1), shift(a, 3)
    b = stack([lax.ppermute(latent, ("yl", "z"), behind), lax.ppermute(other, ("yl", "z"), behind)])
    bl, br = shift(b, 1), shift(b, 3)
    af, bf = shift(al, 1), shift(br, 3)

    w00 = stack([chunks[0]] + arrived, (latent, rest))
    w10 = swap(w00, "yl")
    w01 = swap(w00, "c")
    w11 = swap(w10, "c")
    packed = partial_weights(at, (w00, w01, w10, w11), mine, rest, norm_gain[None], speaker_table, (a,))
    packed = lax.all_to_all(packed, "z", 0, 0, tiled=True)
    give = give_term(at, latent, embed, (b,))
    m, lines = sum_weights(packed, (al, ar, give))
    m00 = lax.all_to_all(m, "z", 0, 0, tiled=True).reshape(256, 768)
    m10 = swap(m00, "yl")
    m01 = swap(m00, "c")
    m11 = swap(m10, "c")

    bounds = jnp.cumsum(turn_lengths, axis=1)
    start = ((row - 1 + jnp.arange(2)[:, None]) * 8 + 2 * jnp.arange(4)[None, :] + core) * BLOCK
    frames = start.reshape(8, 1) + jnp.arange(BLOCK)
    turn = jnp.sum((bounds[:, :, None, None] <= frames[None, None]).astype(jnp.int32), axis=1)
    active = (turn % 2 == 1).astype(F32)

    got = swap(give, "tp")
    embedded, square = embed_rows(at, latent, embed, got, active, speaker_table)
    square = square + swap(square, "tp")
    scale = lax.rsqrt(square[0:1] * (1.0 / D) + 1e-05)
    scale = jnp.concatenate([lax.ppermute(scale, ("yl", "z"), behind), scale])
    scales = [scale] + [shift(scale, 4 - dx) for dx in (1, 2, 3)]

    kv, half = (4, BLOCK, 512), (4, BLOCK, 256)
    side = (active, *scales)
    om, q, whole = project(project_own_kernel, (kv, half, (1024, 768)), at, a, al, ar, af, m00, m01, m10, m11, lines, *side)
    ot = swap(om, "c")
    (pm,) = project(project_prev_kernel, (kv,), at, b, bl, br, bf, whole, lines, *side)
    pt = swap(pm, "c")

    place = jnp.stack([x_at, core, (row == 0).astype(jnp.int32)]).astype(jnp.int32)
    parts = [None] * 4
    for dx in (2, 1, 3, 0):
        part = attention(place, dx, q, om, ot, pm, pt)
        parts[dx] = shift(part, dx) if dx else part
    return embedded, collect(place, parts)


def solution(mesh):
    fine = Mesh(mesh.devices.reshape(2, 8, 4, 2, 2), CTX + ("tp",))
    placed = (
        P("tp", CTX, None),
        P("tp", None, None, None),
        P("tp", None, None),
        P("tp", None, None, None),
        P("tp", None, None),
        P(),
        P(),
        P(),
        P(None, CTX, "tp"),
    )
    return jax.shard_map(
        on_device,
        mesh=fine,
        in_specs=placed,
        out_specs=(P(CTX, "tp"), P(CTX, "tp")),
        check_vma=False,
    )
```

```python
import functools

import jax
import jax.numpy as jnp
from jax import lax
from jax.experimental import pallas as pl
from jax.experimental.pallas import tpu as pltpu
from jax.sharding import Mesh, PartitionSpec as P

HD = 128
BLOCK = 256
D = 4096
CH = 512
CTX = ("yl", "z", "x", "c")
ROW = ("x", "c")
SWAP = [(0, 1), (1, 0)]
BF = jnp.bfloat16
F32 = jnp.float32
LOG2E = 1.4426950408889634
NO_COST = pl.CostEstimate(flops=0, bytes_accessed=0, transcendentals=0)


def elu(v):
    return jnp.where(v > 0, v, jnp.exp(jnp.minimum(v, 0.0)) - 1.0)


def dot(a, b):
    return jnp.dot(a, b, preferred_element_type=F32)


def in_vmem(n):
    return [pl.BlockSpec(memory_space=pltpu.VMEM)] * n


def params(mib):
    return pltpu.CompilerParams(vmem_limit_bytes=mib * 1024 * 1024)


def encoder_kernel(halo_ref, audio_ref, taps_ref, back_ref, down_ref, out_ref, u_ref, e_ref):
    u_ref[0:8, :] = jnp.zeros((8, CH), F32)
    u_ref[8:16, :] = elu(halo_ref[...].astype(F32))
    u_ref[16:, :] = elu(audio_ref[...].astype(F32))
    rows = audio_ref.shape[0] + 8
    inner = dot(u_ref[2 : 2 + rows, :].astype(BF), taps_ref[0])
    inner += dot(u_ref[5 : 5 + rows, :].astype(BF), taps_ref[1])
    inner += dot(u_ref[8 : 8 + rows, :].astype(BF), taps_ref[2])
    hidden = elu(inner).astype(BF)
    branch = dot(hidden, back_ref[...])
    first = (halo_ref[...].astype(F32) + branch[0:8]).astype(BF)
    first = elu(first.astype(F32)).astype(BF).astype(F32)
    rest = (audio_ref[...].astype(F32) + branch[8:]).astype(BF)
    rest = elu(rest.astype(F32)).astype(BF).astype(F32)
    for j in range(CH // 128):
        e_ref[j, 0:8, :] = first[:, j * 128 : (j + 1) * 128]
        e_ref[j, 8:, :] = rest[:, j * 128 : (j + 1) * 128]
    acc = jnp.zeros((BLOCK, CH), F32)
    for k in range(4):
        e = [e_ref[j, pl.ds(6 + k, BLOCK, stride=2), :].astype(BF) for j in range(CH // 128)]
        acc += dot(jnp.concatenate(e, axis=1), down_ref[k])
    out_ref[...] = acc.astype(BF)


def encoder(halo, audio, taps, back, down):
    return pl.pallas_call(
        encoder_kernel,
        in_specs=in_vmem(5),
        out_specs=pl.BlockSpec(memory_space=pltpu.VMEM),
        out_shape=jax.ShapeDtypeStruct((BLOCK, CH), BF),
        scratch_shapes=[pltpu.VMEM((528, CH), F32), pltpu.VMEM((CH // 128, 520, 128), F32)],
        compiler_params=params(20),
        cost_estimate=NO_COST,
    )(halo, audio, taps, back, down)


def swap(a, axis):
    return lax.ppermute(a, axis, SWAP)


def shift(a, by):
    return lax.ppermute(a, "x", [(i, (i + by) % 4) for i in range(4)])


def split_kernel(at_ref, w_ref, near_ref, far_ref, *outs):
    x = at_ref[3]
    for dx in range(4):
        lanes = pl.ds(pl.multiple_of(lax.rem(x + dx, 4) * 256, 256), 256)
        outs[dx][...] = w_ref[:, :, lanes]
    outs[4][0] = near_ref[...]
    outs[4][1] = far_ref[...]


def split(at, w, embed):
    whole = lambda shape: pl.BlockSpec(shape, lambda i, at: (0,) * len(shape))
    return pl.pallas_call(
        split_kernel,
        grid_spec=pltpu.PrefetchScalarGridSpec(
            num_scalar_prefetch=1,
            grid=(1,),
            in_specs=[
                whole((3, 32, 1024)),
                pl.BlockSpec((128, 256), lambda i, at: (at[2], at[0])),
                pl.BlockSpec((128, 256), lambda i, at: (at[2], at[1])),
            ],
            out_specs=[whole((3, 32, 256))] * 4 + [whole((2, 128, 256))],
        ),
        out_shape=[jax.ShapeDtypeStruct((3, 32, 256), BF)] * 4 + [jax.ShapeDtypeStruct((2, 128, 256), BF)],
    )(at, w, embed, embed)


def unused(after):
    return in_vmem(len(after))


def stack_kernel(n, *refs):
    for i in range(n):
        refs[-1][i] = refs[i][...]


def stack(parts, after=()):
    return pl.pallas_call(
        functools.partial(stack_kernel, len(parts)),
        in_specs=in_vmem(len(parts)) + unused(after),
        out_specs=pl.BlockSpec(memory_space=pltpu.VMEM),
        out_shape=jax.ShapeDtypeStruct((len(parts),) + parts[0].shape, parts[0].dtype),
        compiler_params=params(4),
        cost_estimate=NO_COST,
    )(*parts, *after)


def partial_kernel(at_ref, w00, w01, w10, w11, mine_ref, rest_ref, g0, g1, t0, t1, *refs):
    out_ref, w_ref = refs[-2:]
    x, core = at_ref[3], at_ref[4]
    for y, pair in enumerate(((w00, w01), (w10, w11))):
        for c, ref in enumerate(pair):
            for dx in range(4):
                row = lax.rem(x + 4 - dx, 4) * 64 + (core ^ c) * 32
                for j in range(3):
                    w_ref[y, pl.ds(pl.multiple_of(row, 32), 32), j * 256 : (j + 1) * 256] = ref[dx, j]
    part = None
    line = None
    for y, (gain_ref, table_ref) in enumerate(((g0, t0), (g1, t1))):
        w = w_ref[y]
        gain = gain_ref[...]
        embed = jnp.concatenate([mine_ref[y], rest_ref[y]], axis=0).astype(F32) * gain
        table = jnp.concatenate([table_ref[...], jnp.zeros((6, 256), F32)], axis=0) * gain
        high = table.astype(BF)
        low = (table - high.astype(F32)).astype(BF)
        a = dot(embed.astype(BF), w)
        b = dot(high, w) + dot(low, w)
        part = a if part is None else part + a
        line = b if line is None else line + b
    top = line.astype(BF).astype(F32)
    rem = line - top
    rows = [v[s : s + 1, k * 128 : (k + 1) * 128] for v in (top, rem) for s in range(2) for k in range(6)]
    tail = jnp.concatenate(rows + [jnp.zeros((8, 128), F32)], axis=0).astype(BF)
    for i in range(8):
        out_ref[i, :, 0:768] = part[i * 32 : (i + 1) * 32].astype(BF)
        out_ref[i, :, 768:896] = tail


def partial_weights(at, ws, mine, rest, gain, table, after):
    whole = lambda shape: pl.BlockSpec(shape, lambda i, at: (0,) * len(shape))
    here = lambda rows, k: pl.BlockSpec((rows, 256), lambda i, at: (0, at[k]))
    return pl.pallas_call(
        partial_kernel,
        grid_spec=pltpu.PrefetchScalarGridSpec(
            num_scalar_prefetch=1,
            grid=(1,),
            in_specs=[whole((4, 3, 32, 256))] * 4
            + [whole((2, 128, 256))] * 2
            + [here(1, 0), here(1, 1), here(2, 0), here(2, 1)]
            + unused(after),
            out_specs=whole((8, 32, 896)),
            scratch_shapes=[pltpu.VMEM((2, 256, 768), BF)],
        ),
        out_shape=jax.ShapeDtypeStruct((8, 32, 896), BF),
        compiler_params=params(16),
        cost_estimate=NO_COST,
    )(at, *ws, mine, rest, gain, gain, table, table, *after)


def sum_kernel(p_ref, *refs):
    m_ref, line_ref = refs[-2:]
    total = jnp.sum(p_ref[...].astype(F32), axis=0)
    m = total[:, :768].astype(BF)
    for i in range(8):
        m_ref[i] = m
    both = total[0:12, 768:] + total[12:24, 768:]
    line_ref[...] = jnp.zeros((8, 768), F32)
    for s in range(2):
        for k in range(6):
            line_ref[s : s + 1, k * 128 : (k + 1) * 128] = both[s * 6 + k : s * 6 + k + 1]


def sum_weights(packed, after):
    return pl.pallas_call(
        sum_kernel,
        in_specs=in_vmem(1) + unused(after),
        out_specs=in_vmem(2),
        out_shape=[jax.ShapeDtypeStruct((8, 32, 768), BF), jax.ShapeDtypeStruct((8, 768), F32)],
        compiler_params=params(8),
        cost_estimate=NO_COST,
    )(packed, *after)


def term_kernel(at_ref, latent_ref, embed_ref, *refs):
    give_ref, own_ref = refs[-2:]
    term = dot(latent_ref[...], embed_ref[...])
    mine = at_ref[5] == pl.program_id(0) // 2

    @pl.when(mine)
    def _():
        own_ref[...] = term

    @pl.when(jnp.logical_not(mine))
    def _():
        give_ref[...] = term.astype(BF)


def terms(at, latent, embed, after):
    def give_at(i, at):
        return (0, jnp.where(at[5] == 0, jnp.maximum(i - 2, 0), jnp.minimum(i, 1)))

    def own_at(i, at):
        return (0, jnp.where(at[5] == 1, jnp.maximum(i - 2, 0), jnp.minimum(i, 1)))

    return pl.pallas_call(
        term_kernel,
        grid_spec=pltpu.PrefetchScalarGridSpec(
            num_scalar_prefetch=1,
            grid=(4,),
            in_specs=[pl.BlockSpec((BLOCK, CH), lambda i, at: (0, 0)), pl.BlockSpec((CH, 1024), lambda i, at: (0, i))]
            + unused(after),
            out_specs=[pl.BlockSpec((BLOCK, 1024), give_at), pl.BlockSpec((BLOCK, 1024), own_at)],
        ),
        out_shape=[jax.ShapeDtypeStruct((BLOCK, D // 2), BF), jax.ShapeDtypeStruct((BLOCK, D // 2), F32)],
        compiler_params=params(16),
        cost_estimate=NO_COST,
    )(at, latent, embed, *after)


def embed_kernel(at_ref, own_ref, got_ref, active_ref, table_ref, out_ref, square_ref):
    act = active_ref[:, pl.ds(at_ref[3] + 4, 1), :].reshape(2, BLOCK)
    cols = jnp.concatenate([act, jnp.zeros((6, BLOCK), F32)], axis=0).T
    x = own_ref[...] + got_ref[...].astype(F32)
    x = x + cols[:, 0:1] * table_ref[0:1] + cols[:, 1:2] * table_ref[1:2]
    out_ref[...] = x.astype(BF)
    square = jnp.sum(x * x, axis=1, keepdims=True)
    square = jnp.broadcast_to(square, (BLOCK, 128)).T[0:8]

    @pl.when(pl.program_id(0) == 0)
    def _():
        square_ref[...] = square

    @pl.when(pl.program_id(0) != 0)
    def _():
        square_ref[...] += square


def embed_rows(at, own, got, active, table):
    tile = pl.BlockSpec((BLOCK, 1024), lambda i, at: (0, i))
    return pl.pallas_call(
        embed_kernel,
        grid_spec=pltpu.PrefetchScalarGridSpec(
            num_scalar_prefetch=1,
            grid=(2,),
            in_specs=[
                tile,
                tile,
                pl.BlockSpec((2, 8, BLOCK), lambda i, at: (0, 0, 0)),
                pl.BlockSpec((2, 1024), lambda i, at: (0, at[5] * 2 + i)),
            ],
            out_specs=[tile, pl.BlockSpec((8, BLOCK), lambda i, at: (0, 0))],
        ),
        out_shape=[jax.ShapeDtypeStruct((BLOCK, D // 2), BF), jax.ShapeDtypeStruct((8, BLOCK), F32)],
        compiler_params=params(16),
        cost_estimate=NO_COST,
    )(at, own, got, active, table)


def project_rows(row, blocks, m_ref, line_ref, active_ref, at_ref, kv_ref, q_ref):
    x = at_ref[3]
    cols = slice(0, 768) if q_ref is not None else slice(256, 768)
    w0, w1 = m_ref[0:512, cols], m_ref[512:1024, cols]
    line = line_ref[:, cols]
    for dx in range(4):
        at = lax.rem(x + dx, 4)
        act = active_ref[:, pl.ds(4 * row + at, 1), :].reshape(2, BLOCK)
        side = jnp.concatenate([act, jnp.zeros((6, BLOCK), F32)], axis=0).T
        acc = dot(blocks[dx][0], w0) + dot(blocks[dx][1], w1)
        acc = acc + side[:, 0:1] * line[0:1] + side[:, 1:2] * line[1:2]
        kv_ref[at] = acc[:, -512:].astype(BF)
        if q_ref is not None:
            q_ref[at] = acc[:, :256]


def project_own_kernel(at_ref, a, al, ar, af, m00, m01, m10, m11, line_ref, active_ref, kv_ref, q_ref, m_ref):
    core, yl = at_ref[4], at_ref[6]
    for y, pair in enumerate(((m00, m01), (m10, m11))):
        for c, ref in enumerate(pair):
            row = ((yl ^ y) * 2 + (core ^ c)) * 128
            for s in range(2):
                m_ref[pl.ds(pl.multiple_of(s * 512 + row, 128), 128), :] = ref[s * 128 : (s + 1) * 128, :]
    project_rows(1, (a, ar, af, al), m_ref, line_ref, active_ref, at_ref, kv_ref, q_ref)


def project_prev_kernel(at_ref, b, bl, br, bf, m_ref, line_ref, active_ref, after_ref, kv_ref):
    project_rows(0, (b, br, bf, bl), m_ref, line_ref, active_ref, at_ref, kv_ref, None)


def project(kernel, outs, *args):
    return pl.pallas_call(
        kernel,
        in_specs=[pl.BlockSpec(memory_space=pltpu.SMEM)] + in_vmem(len(args) - 1),
        out_specs=in_vmem(len(outs)),
        out_shape=outs,
        compiler_params=params(10),
        cost_estimate=NO_COST,
    )(*args)


def attention_kernel(place_ref, q_ref, om_ref, ot_ref, pm_ref, pt_ref, own_ref, prev_ref, o_ref):
    at = lax.rem(place_ref[0] + place_ref[3], 4)
    core = place_ref[1]
    first = place_ref[2]
    rows = lax.broadcasted_iota(jnp.int32, (BLOCK, BLOCK), 0)
    cols = lax.broadcasted_iota(jnp.int32, (BLOCK, BLOCK), 1)
    blocks = []
    for kv_own, kv_prev, begin, parity in ((om_ref, pm_ref, at + 1, core), (ot_ref, pt_ref, at + core, 1 - core)):
        for j in range(4):
            m = begin + j
            i = lax.rem(m, 4)
            kv = jnp.where(m >= 4, kv_own[i], kv_prev[i])
            factor = jnp.where(m >= 4, own_ref[pl.ds(2 * i + parity, 1), :], prev_ref[pl.ds(2 * i + parity, 1), :])
            blocks.append((kv, factor, jnp.where((m < 4) & (first == 1), 1e30, 0.0)))
    mine = jnp.broadcast_to(own_ref[pl.ds(2 * at + core, 1), :] * (HD**-0.5 * LOG2E), (8, BLOCK)).T[:, 0:1]
    contract = (((1,), (1,)), ((), ()))
    for h in range(2):
        q = (q_ref[at, :, h * HD : (h + 1) * HD] * mine).astype(BF)
        scores = []
        top = None
        for n, (kv, factor, penalty) in enumerate(blocks):
            s = lax.dot_general(q, kv[:, h * HD : (h + 1) * HD], contract, preferred_element_type=F32) * factor
            if n == 3:
                s = jnp.where(cols <= rows, s, -1e30)
            if n == 4:
                s = jnp.where(cols > rows, s, -1e30)
            most = jnp.max(s, axis=1, keepdims=True) - penalty
            top = most if top is None else jnp.maximum(top, most)
            scores.append(s)
        total = jnp.zeros((BLOCK, 1), F32)
        o = jnp.zeros((BLOCK, HD), F32)
        for s, (kv, factor, penalty) in zip(scores, blocks):
            p = jnp.exp2(s - (top + penalty))
            total += jnp.sum(p, axis=1, keepdims=True)
            o += dot((p * factor).astype(BF), kv[:, 256 + h * HD : 256 + (h + 1) * HD])
        o_ref[0, :, h * HD : (h + 1) * HD] = (o / total).astype(BF)


def attention(place, dx, *args):
    return pl.pallas_call(
        attention_kernel,
        in_specs=[pl.BlockSpec(memory_space=pltpu.SMEM)] + in_vmem(7),
        out_specs=pl.BlockSpec(memory_space=pltpu.VMEM),
        out_shape=jax.ShapeDtypeStruct((1, BLOCK, 256), BF),
        compiler_params=params(8),
        cost_estimate=NO_COST,
    )(jnp.concatenate([place, jnp.array([dx], jnp.int32)]), *args)


def collect_kernel(place_ref, a_ref, b_ref, c_ref, d_ref, o_ref):
    for dx, ref in enumerate((a_ref, b_ref, c_ref, d_ref)):
        at = lax.rem(place_ref[0] + 4 - dx, 4)
        o_ref[:, pl.ds(pl.multiple_of(at * 256, 256), 256)] = ref[0]


def collect(place, parts):
    return pl.pallas_call(
        collect_kernel,
        in_specs=[pl.BlockSpec(memory_space=pltpu.SMEM)] + in_vmem(4),
        out_specs=pl.BlockSpec(memory_space=pltpu.VMEM),
        out_shape=jax.ShapeDtypeStruct((BLOCK, 1024), BF),
        compiler_params=params(20),
    )(place, *parts)


def on_device(
    audio_feats,
    res_conv,
    res_out,
    down_conv,
    stream_embed,
    turn_lengths,
    speaker_table,
    norm_gain,
    qkv_weight,
):
    tp = lax.axis_index("tp")
    x_at = lax.axis_index("x")
    core = lax.axis_index("c")
    yl = lax.axis_index("yl")
    z = lax.axis_index("z")
    row = yl * 8 + z
    at = jnp.stack([yl * 8 + z, (1 - yl) * 8 + z, yl * 2 + core, x_at, core, tp, yl]).astype(jnp.int32)
    behind = [(i, i + 1) for i in range(15)]

    audio = audio_feats[0]
    halo = lax.ppermute(audio[-8:], CTX, [(i, i + 1) for i in range(127)])
    embed = stream_embed[0]
    *chunks, mine = split(at, qkv_weight, embed)
    arrived = [shift(chunks[dx], dx) for dx in (1, 2, 3)]
    rest = swap(mine, "tp")

    latent = encoder(halo, audio, res_conv[0], res_out[0], down_conv[0])
    give, own = terms(at, latent, embed, ())
    other = swap(latent, "tp")
    a = stack([latent, other])
    prev = lax.ppermute(latent, ("yl", "z"), behind)
    b = stack([prev, lax.ppermute(other, ("yl", "z"), behind)])
    al, ar = shift(a, 1), shift(a, 3)
    bl, br = shift(b, 1), shift(b, 3)
    af, bf = shift(al, 1), shift(br, 3)

    w00 = stack([chunks[0]] + arrived, (latent, rest))
    w10 = swap(w00, "yl")
    w01 = swap(w00, "c")
    w11 = swap(w10, "c")
    packed = partial_weights(at, (w00, w01, w10, w11), mine, rest, norm_gain[None], speaker_table, (give, a, prev))
    packed = lax.all_to_all(packed, "z", 0, 0, tiled=True)
    m, lines = sum_weights(packed, (al, ar, b))
    bounds = jnp.cumsum(turn_lengths, axis=1)
    start = ((row - 1 + jnp.arange(2)[:, None]) * 8 + 2 * jnp.arange(4)[None, :] + core) * BLOCK
    frames = start.reshape(8, 1) + jnp.arange(BLOCK)
    turn = jnp.sum((bounds[:, :, None, None] <= frames[None, None]).astype(jnp.int32), axis=1)
    active = (turn % 2 == 1).astype(F32)

    got = swap(give, "tp")
    embedded, square = embed_rows(at, own, got, active, speaker_table)
    square = square + swap(square, "tp")
    scale = lax.rsqrt(square[0:1] * (1.0 / D) + 1e-05)
    m00 = lax.all_to_all(m, "z", 0, 0, tiled=True).reshape(256, 768)
    (m00,) = stack([m00], (scale, bl, br))
    m10 = swap(m00, "yl")
    m01 = swap(m00, "c")
    scales = lax.all_to_all(jnp.broadcast_to(scale, (8, BLOCK)), ROW, 0, 0, tiled=True)
    (m10,) = stack([m10], (scales,))
    m11 = swap(m10, "c")
    scales_prev = lax.ppermute(scales, ("yl", "z"), behind)

    kv = jax.ShapeDtypeStruct((4, BLOCK, 512), BF)
    half = jax.ShapeDtypeStruct((4, BLOCK, 256), F32)
    full = jax.ShapeDtypeStruct((1024, 768), BF)
    om, q, whole = project(
        project_own_kernel, (kv, half, full), at, a, al, ar, af, m00, m01, m10, m11, lines, active
    )
    ot = swap(om, "c")
    (pm,) = project(project_prev_kernel, (kv,), at, b, bl, br, bf, whole, lines, active, scales_prev)
    pt = swap(pm, "c")

    place = jnp.stack([x_at, core, (row == 0).astype(jnp.int32)]).astype(jnp.int32)
    parts = [None] * 4
    for dx in (2, 1, 3, 0):
        part = attention(place, dx, q, om, ot, pm, pt, scales, scales_prev)
        parts[dx] = shift(part, dx) if dx else part
    return embedded, collect(place, parts)


def solution(mesh):
    fine = Mesh(mesh.devices.reshape(2, 8, 4, 2, 2), CTX + ("tp",))
    placed = (
        P("tp", CTX, None),
        P("tp", None, None, None),
        P("tp", None, None),
        P("tp", None, None, None),
        P("tp", None, None),
        P(),
        P(),
        P(),
        P(None, CTX, "tp"),
    )
    return jax.shard_map(
        on_device,
        mesh=fine,
        in_specs=placed,
        out_specs=(P(CTX, "tp"), P(CTX, "tp")),
        check_vma=False,
    )
```

```python
import functools

import jax
import jax.numpy as jnp
from jax import lax
from jax.experimental import pallas as pl
from jax.experimental.pallas import tpu as pltpu
from jax.sharding import Mesh, PartitionSpec as P

HD = 128
BLOCK = 256
D = 4096
CH = 512
CTX = ("yl", "z", "x", "c")
SWAP = [(0, 1), (1, 0)]
BF = jnp.bfloat16
F32 = jnp.float32
LOG2E = 1.4426950408889634
NO_COST = pl.CostEstimate(flops=0, bytes_accessed=0, transcendentals=0)


def elu(v):
    return jnp.where(v > 0, v, jnp.exp(jnp.minimum(v, 0.0)) - 1.0)


def dot(a, b):
    return jnp.dot(a, b, preferred_element_type=F32)


def in_vmem(n):
    return [pl.BlockSpec(memory_space=pltpu.VMEM)] * n


def params(mib):
    return pltpu.CompilerParams(vmem_limit_bytes=mib * 1024 * 1024)


def encoder_kernel(halo_ref, audio_ref, taps_ref, back_ref, down_ref, out_ref, u_ref, e_ref):
    u_ref[0:8, :] = jnp.zeros((8, CH), F32)
    u_ref[8:16, :] = elu(halo_ref[...].astype(F32))
    u_ref[16:, :] = elu(audio_ref[...].astype(F32))
    rows = audio_ref.shape[0] + 8
    inner = dot(u_ref[2 : 2 + rows, :].astype(BF), taps_ref[0])
    inner += dot(u_ref[5 : 5 + rows, :].astype(BF), taps_ref[1])
    inner += dot(u_ref[8 : 8 + rows, :].astype(BF), taps_ref[2])
    hidden = elu(inner).astype(BF)
    branch = dot(hidden, back_ref[...])
    first = (halo_ref[...].astype(F32) + branch[0:8]).astype(BF)
    first = elu(first.astype(F32)).astype(BF).astype(F32)
    rest = (audio_ref[...].astype(F32) + branch[8:]).astype(BF)
    rest = elu(rest.astype(F32)).astype(BF).astype(F32)
    for j in range(CH // 128):
        e_ref[j, 0:8, :] = first[:, j * 128 : (j + 1) * 128]
        e_ref[j, 8:, :] = rest[:, j * 128 : (j + 1) * 128]
    acc = jnp.zeros((BLOCK, CH), F32)
    for k in range(4):
        e = [e_ref[j, pl.ds(6 + k, BLOCK, stride=2), :].astype(BF) for j in range(CH // 128)]
        acc += dot(jnp.concatenate(e, axis=1), down_ref[k])
    out_ref[...] = acc.astype(BF)


def encoder(halo, audio, taps, back, down):
    return pl.pallas_call(
        encoder_kernel,
        in_specs=in_vmem(5),
        out_specs=pl.BlockSpec(memory_space=pltpu.VMEM),
        out_shape=jax.ShapeDtypeStruct((BLOCK, CH), BF),
        scratch_shapes=[pltpu.VMEM((528, CH), F32), pltpu.VMEM((CH // 128, 520, 128), F32)],
        compiler_params=params(20),
        cost_estimate=NO_COST,
    )(halo, audio, taps, back, down)


def swap(a, axis):
    return lax.ppermute(a, axis, SWAP)


def shift(a, by):
    return lax.ppermute(a, "x", [(i, (i + by) % 4) for i in range(4)])


def split_kernel(at_ref, w_ref, near_ref, far_ref, *outs):
    x = at_ref[3]
    for dx in range(4):
        lanes = pl.ds(pl.multiple_of(lax.rem(x + dx, 4) * 256, 256), 256)
        outs[dx][...] = w_ref[:, :, lanes]
    outs[4][0] = near_ref[...]
    outs[4][1] = far_ref[...]


def split(at, w, embed):
    whole = lambda shape: pl.BlockSpec(shape, lambda i, at: (0,) * len(shape))
    return pl.pallas_call(
        split_kernel,
        grid_spec=pltpu.PrefetchScalarGridSpec(
            num_scalar_prefetch=1,
            grid=(1,),
            in_specs=[
                whole((3, 32, 1024)),
                pl.BlockSpec((128, 256), lambda i, at: (at[2], at[0])),
                pl.BlockSpec((128, 256), lambda i, at: (at[2], at[1])),
            ],
            out_specs=[whole((3, 32, 256))] * 4 + [whole((2, 128, 256))],
        ),
        out_shape=[jax.ShapeDtypeStruct((3, 32, 256), BF)] * 4 + [jax.ShapeDtypeStruct((2, 128, 256), BF)],
    )(at, w, embed, embed)


def unused(after):
    return in_vmem(len(after))


def stack_kernel(n, *refs):
    for i in range(n):
        refs[-1][i] = refs[i][...]


def stack(parts, after=()):
    return pl.pallas_call(
        functools.partial(stack_kernel, len(parts)),
        in_specs=in_vmem(len(parts)) + unused(after),
        out_specs=pl.BlockSpec(memory_space=pltpu.VMEM),
        out_shape=jax.ShapeDtypeStruct((len(parts),) + parts[0].shape, parts[0].dtype),
        compiler_params=params(4),
        cost_estimate=NO_COST,
    )(*parts, *after)


def partial_kernel(at_ref, w00, w01, w10, w11, mine_ref, rest_ref, g0, g1, t0, t1, *refs):
    out_ref, w_ref = refs[-2:]
    x, core = at_ref[3], at_ref[4]
    for y, pair in enumerate(((w00, w01), (w10, w11))):
        for c, ref in enumerate(pair):
            for dx in range(4):
                row = lax.rem(x + 4 - dx, 4) * 64 + (core ^ c) * 32
                for j in range(3):
                    w_ref[y, pl.ds(pl.multiple_of(row, 32), 32), j * 256 : (j + 1) * 256] = ref[dx, j]
    part = None
    line = None
    for y, (gain_ref, table_ref) in enumerate(((g0, t0), (g1, t1))):
        w = w_ref[y]
        gain = gain_ref[...]
        embed = jnp.concatenate([mine_ref[y], rest_ref[y]], axis=0).astype(F32) * gain
        table = jnp.concatenate([table_ref[...], jnp.zeros((6, 256), F32)], axis=0) * gain
        high = table.astype(BF)
        low = (table - high.astype(F32)).astype(BF)
        a = dot(embed.astype(BF), w)
        b = dot(high, w) + dot(low, w)
        part = a if part is None else part + a
        line = b if line is None else line + b
    top = line.astype(BF).astype(F32)
    rem = line - top
    rows = [v[s : s + 1, k * 128 : (k + 1) * 128] for v in (top, rem) for s in range(2) for k in range(6)]
    tail = jnp.concatenate(rows + [jnp.zeros((8, 128), F32)], axis=0).astype(BF)
    for i in range(8):
        out_ref[i, :, 0:768] = part[i * 32 : (i + 1) * 32].astype(BF)
        out_ref[i, :, 768:896] = tail


def partial_weights(at, ws, mine, rest, gain, table, after):
    whole = lambda shape: pl.BlockSpec(shape, lambda i, at: (0,) * len(shape))
    here = lambda rows, k: pl.BlockSpec((rows, 256), lambda i, at: (0, at[k]))
    return pl.pallas_call(
        partial_kernel,
        grid_spec=pltpu.PrefetchScalarGridSpec(
            num_scalar_prefetch=1,
            grid=(1,),
            in_specs=[whole((4, 3, 32, 256))] * 4
            + [whole((2, 128, 256))] * 2
            + [here(1, 0), here(1, 1), here(2, 0), here(2, 1)]
            + unused(after),
            out_specs=whole((8, 32, 896)),
            scratch_shapes=[pltpu.VMEM((2, 256, 768), BF)],
        ),
        out_shape=jax.ShapeDtypeStruct((8, 32, 896), BF),
        compiler_params=params(16),
        cost_estimate=NO_COST,
    )(at, *ws, mine, rest, gain, gain, table, table, *after)


def sum_kernel(p_ref, *refs):
    m_ref, line_ref = refs[-2:]
    total = jnp.sum(p_ref[...].astype(F32), axis=0)
    m = total[:, :768].astype(BF)
    for i in range(8):
        m_ref[i] = m
    both = total[0:12, 768:] + total[12:24, 768:]
    line_ref[...] = jnp.zeros((8, 768), F32)
    for s in range(2):
        for k in range(6):
            line_ref[s : s + 1, k * 128 : (k + 1) * 128] = both[s * 6 + k : s * 6 + k + 1]


def sum_weights(packed, after):
    return pl.pallas_call(
        sum_kernel,
        in_specs=in_vmem(1) + unused(after),
        out_specs=in_vmem(2),
        out_shape=[jax.ShapeDtypeStruct((8, 32, 768), BF), jax.ShapeDtypeStruct((8, 768), F32)],
        compiler_params=params(8),
        cost_estimate=NO_COST,
    )(packed, *after)


def term_kernel(at_ref, latent_ref, embed_ref, *refs):
    give_ref, own_ref = refs[-2:]
    term = dot(latent_ref[...], embed_ref[...])
    mine = at_ref[5] == pl.program_id(0) // 2

    @pl.when(mine)
    def _():
        own_ref[...] = term.astype(BF)

    @pl.when(jnp.logical_not(mine))
    def _():
        give_ref[...] = term.astype(BF)


def terms(at, latent, embed, after):
    def give_at(i, at):
        return (0, jnp.where(at[5] == 0, jnp.maximum(i - 2, 0), jnp.minimum(i, 1)))

    def own_at(i, at):
        return (0, jnp.where(at[5] == 1, jnp.maximum(i - 2, 0), jnp.minimum(i, 1)))

    return pl.pallas_call(
        term_kernel,
        grid_spec=pltpu.PrefetchScalarGridSpec(
            num_scalar_prefetch=1,
            grid=(4,),
            in_specs=[pl.BlockSpec((BLOCK, CH), lambda i, at: (0, 0)), pl.BlockSpec((CH, 1024), lambda i, at: (0, i))]
            + unused(after),
            out_specs=[pl.BlockSpec((BLOCK, 1024), give_at), pl.BlockSpec((BLOCK, 1024), own_at)],
        ),
        out_shape=[jax.ShapeDtypeStruct((BLOCK, D // 2), BF)] * 2,
        compiler_params=params(16),
        cost_estimate=NO_COST,
    )(at, latent, embed, *after)


def embed_kernel(at_ref, own_ref, got_ref, active_ref, table_ref, *refs):
    out_ref, square_ref = refs[-2:]
    act = active_ref[:, pl.ds(at_ref[3] + 4, 1), :].reshape(2, BLOCK)
    cols = jnp.concatenate([act, jnp.zeros((6, BLOCK), F32)], axis=0).T
    x = own_ref[...].astype(F32) + got_ref[...].astype(F32)
    x = x + cols[:, 0:1] * table_ref[0:1] + cols[:, 1:2] * table_ref[1:2]
    out_ref[...] = x.astype(BF)
    square = jnp.sum(x * x, axis=1, keepdims=True)
    square = jnp.broadcast_to(square, (BLOCK, 128)).T[0:8]

    @pl.when(pl.program_id(0) == 0)
    def _():
        square_ref[...] = square

    @pl.when(pl.program_id(0) != 0)
    def _():
        square_ref[...] += square


def embed_rows(at, own, got, active, table, after):
    tile = pl.BlockSpec((BLOCK, 1024), lambda i, at: (0, i))
    return pl.pallas_call(
        embed_kernel,
        grid_spec=pltpu.PrefetchScalarGridSpec(
            num_scalar_prefetch=1,
            grid=(2,),
            in_specs=[
                tile,
                tile,
                pl.BlockSpec((2, 8, BLOCK), lambda i, at: (0, 0, 0)),
                pl.BlockSpec((2, 1024), lambda i, at: (0, at[5] * 2 + i)),
            ]
            + unused(after),
            out_specs=[tile, pl.BlockSpec((8, BLOCK), lambda i, at: (0, 0))],
        ),
        out_shape=[jax.ShapeDtypeStruct((BLOCK, D // 2), BF), jax.ShapeDtypeStruct((8, BLOCK), F32)],
        compiler_params=params(16),
        cost_estimate=pl.CostEstimate(flops=20000000000, bytes_accessed=0, transcendentals=0),
    )(at, own, got, active, table, *after)


def project_rows(row, blocks, m_ref, line_ref, active_ref, scale_ref, at_ref, kv_ref, q_ref):
    x = at_ref[3]
    cols = slice(0, 768) if q_ref is not None else slice(256, 768)
    w0, w1 = m_ref[0:512, cols], m_ref[512:1024, cols]
    line = line_ref[:, cols]
    for dx in range(4):
        at = lax.rem(x + dx, 4)
        act = active_ref[:, pl.ds(4 * row + at, 1), :].reshape(2, BLOCK)
        side = jnp.concatenate([act, scale_ref[pl.ds(at, 1), :], jnp.zeros((5, BLOCK), F32)], axis=0).T
        acc = dot(blocks[dx][0], w0) + dot(blocks[dx][1], w1)
        acc = (acc + side[:, 0:1] * line[0:1] + side[:, 1:2] * line[1:2]) * side[:, 2:3]
        kv_ref[at] = acc[:, -512:].astype(BF)
        if q_ref is not None:
            q_ref[at] = (acc[:, :256] * (HD**-0.5 * LOG2E)).astype(BF)


def project_own_kernel(at_ref, a, al, ar, af, m00, m01, m10, m11, line_ref, active_ref, scale_ref, kv_ref, q_ref, m_ref):
    core, yl = at_ref[4], at_ref[6]
    for y, pair in enumerate(((m00, m01), (m10, m11))):
        for c, ref in enumerate(pair):
            row = ((yl ^ y) * 2 + (core ^ c)) * 128
            for s in range(2):
                m_ref[pl.ds(pl.multiple_of(s * 512 + row, 128), 128), :] = ref[s * 128 : (s + 1) * 128, :]
    project_rows(1, (a, ar, af, al), m_ref, line_ref, active_ref, scale_ref, at_ref, kv_ref, q_ref)


def project_prev_kernel(at_ref, b, bl, br, bf, m_ref, line_ref, active_ref, scale_ref, kv_ref):
    project_rows(0, (b, br, bf, bl), m_ref, line_ref, active_ref, scale_ref, at_ref, kv_ref, None)


def project(kernel, outs, *args):
    return pl.pallas_call(
        kernel,
        in_specs=[pl.BlockSpec(memory_space=pltpu.SMEM)] + in_vmem(len(args) - 1),
        out_specs=in_vmem(len(outs)),
        out_shape=outs,
        compiler_params=params(10),
        cost_estimate=NO_COST,
    )(*args)


def attention_kernel(n, place_ref, q_ref, om_ref, ot_ref, pm_ref, pt_ref, *o_refs):
    x, core, first = place_ref[0], place_ref[1], place_ref[2]
    half = BLOCK // 2
    cols = lax.broadcasted_iota(jnp.int32, (half, BLOCK), 1)
    ones = jnp.ones((8 * BLOCK, HD), BF)
    contract = (((1,), (1,)), ((), ()))
    for step in range(n):
        at = lax.rem(x + place_ref[3 + step], 4)
        blocks, penalties = [], []
        for own_ref, prev_ref, begin in ((om_ref, pm_ref, at + 1), (ot_ref, pt_ref, at + core)):
            for j in range(4):
                m = begin + j
                i = lax.rem(m, 4)
                blocks.append(jnp.where(m >= 4, own_ref[i], prev_ref[i]))
                penalties.append(jnp.where((m < 4) & (first == 1), 1e30, 0.0))
        kv = jnp.concatenate(blocks, axis=0)
        for h in range(2):
            q = q_ref[at, :, h * HD : (h + 1) * HD]
            k = kv[:, h * HD : (h + 1) * HD]
            v = jnp.concatenate([kv[:, 256 + h * HD : 256 + (h + 1) * HD], ones], axis=1)
            for begin in (0, half):
                rows = lax.broadcasted_iota(jnp.int32, (half, BLOCK), 0) + begin
                s = lax.dot_general(q[begin : begin + half], k, contract, preferred_element_type=F32)
                s = [s[:, j * BLOCK : (j + 1) * BLOCK] for j in range(8)]
                s[3] = jnp.where(cols <= rows, s[3], -1e30)
                s[4] = jnp.where(cols > rows, s[4], -1e30)
                tops = [jnp.max(v, axis=1, keepdims=True) - penalty for v, penalty in zip(s, penalties)]
                top = functools.reduce(jnp.maximum, tops)
                p = [jnp.exp2(v - (top + penalty)).astype(BF) for v, penalty in zip(s, penalties)]
                o = dot(jnp.concatenate(p, axis=1), v)
                o_refs[step][begin : begin + half, h * HD : (h + 1) * HD] = (o[:, :HD] / o[:, HD:]).astype(BF)


def attention(place, offsets, *args):
    n = len(offsets)
    return pl.pallas_call(
        functools.partial(attention_kernel, n),
        in_specs=[pl.BlockSpec(memory_space=pltpu.SMEM)] + in_vmem(5),
        out_specs=in_vmem(n),
        out_shape=[jax.ShapeDtypeStruct((BLOCK, 256), BF)] * n,
        compiler_params=params(16),
        cost_estimate=NO_COST,
    )(jnp.concatenate([place, jnp.array(offsets, jnp.int32)]), *args)


def collect_kernel(place_ref, a_ref, b_ref, c_ref, d_ref, o_ref):
    for dx, ref in enumerate((a_ref, b_ref, c_ref, d_ref)):
        at = lax.rem(place_ref[0] + 4 - dx, 4)
        o_ref[:, pl.ds(pl.multiple_of(at * 256, 256), 256)] = ref[...]


def collect(place, parts):
    return pl.pallas_call(
        collect_kernel,
        in_specs=[pl.BlockSpec(memory_space=pltpu.SMEM)] + in_vmem(4),
        out_specs=pl.BlockSpec(memory_space=pltpu.VMEM),
        out_shape=jax.ShapeDtypeStruct((BLOCK, 1024), BF),
        compiler_params=params(20),
    )(place, *parts)


def on_device(
    audio_feats,
    res_conv,
    res_out,
    down_conv,
    stream_embed,
    turn_lengths,
    speaker_table,
    norm_gain,
    qkv_weight,
):
    tp = lax.axis_index("tp")
    x_at = lax.axis_index("x")
    core = lax.axis_index("c")
    yl = lax.axis_index("yl")
    z = lax.axis_index("z")
    row = yl * 8 + z
    at = jnp.stack([yl * 8 + z, (1 - yl) * 8 + z, yl * 2 + core, x_at, core, tp, yl]).astype(jnp.int32)
    behind = [(i, i + 1) for i in range(15)]

    audio = audio_feats[0]
    halo = lax.ppermute(audio[-8:], CTX, [(i, i + 1) for i in range(127)])
    embed = stream_embed[0]
    *chunks, mine = split(at, qkv_weight, embed)
    arrived = [shift(chunks[dx], dx) for dx in (1, 2, 3)]
    rest = swap(mine, "tp")

    latent = encoder(halo, audio, res_conv[0], res_out[0], down_conv[0])
    give, own = terms(at, latent, embed, ())
    other = swap(latent, "tp")
    a = stack([latent, other])
    prev = lax.ppermute(latent, ("yl", "z"), behind)
    b = stack([prev, lax.ppermute(other, ("yl", "z"), behind)])
    al, ar = shift(a, 1), shift(a, 3)
    bl, br = shift(b, 1), shift(b, 3)
    af, bf = shift(al, 1), shift(br, 3)

    w00 = stack([chunks[0]] + arrived, (latent, rest))
    w10 = swap(w00, "yl")
    w01 = swap(w00, "c")
    w11 = swap(w10, "c")
    packed = partial_weights(at, (w00, w01, w10, w11), mine, rest, norm_gain[None], speaker_table, (give, a, prev))
    packed = lax.all_to_all(packed, "z", 0, 0, tiled=True)
    m, lines = sum_weights(packed, (al, ar))
    bounds = jnp.cumsum(turn_lengths, axis=1)
    start = ((row - 1 + jnp.arange(2)[:, None]) * 8 + 2 * jnp.arange(4)[None, :] + core) * BLOCK
    frames = start.reshape(8, 1) + jnp.arange(BLOCK)
    turn = jnp.sum((bounds[:, :, None, None] <= frames[None, None]).astype(jnp.int32), axis=1)
    active = (turn % 2 == 1).astype(F32)

    got = swap(give, "tp")
    embedded, square = embed_rows(at, own, got, active, speaker_table, ())
    square = square + swap(square, "tp")
    scale = lax.rsqrt(square[0:1] * (1.0 / D) + 1e-05)
    m00 = lax.all_to_all(m, "z", 0, 0, tiled=True).reshape(256, 768)
    (m00,) = stack([m00], (scale, bl, br))
    m10 = swap(m00, "yl")
    m01 = swap(m00, "c")
    scales = lax.all_to_all(jnp.broadcast_to(scale, (4, BLOCK)), "x", 0, 0, tiled=True)
    (m10,) = stack([m10], (scales,))
    m11 = swap(m10, "c")
    scales_prev = lax.ppermute(scales, ("yl", "z"), behind)

    kv = jax.ShapeDtypeStruct((4, BLOCK, 512), BF)
    half = jax.ShapeDtypeStruct((4, BLOCK, 256), BF)
    full = jax.ShapeDtypeStruct((1024, 768), BF)
    om, q, whole = project(
        project_own_kernel, (kv, half, full), at, a, al, ar, af, m00, m01, m10, m11, lines, active, scales
    )
    ot = swap(om, "c")
    (pm,) = project(project_prev_kernel, (kv,), at, b, bl, br, bf, whole, lines, active, scales_prev)
    pt = swap(pm, "c")

    place = jnp.stack([x_at, core, (row == 0).astype(jnp.int32)]).astype(jnp.int32)
    blocks = (q, om, ot, pm, pt)
    sent = (2, 1, 3)
    parts = dict(zip(sent, attention(place, sent, *blocks)))
    parts = {dx: shift(part, dx) for dx, part in parts.items()}
    (parts[0],) = attention(place, (0,), *blocks)
    return embedded, collect(place, [parts[dx] for dx in range(4)])


def solution(mesh):
    fine = Mesh(mesh.devices.reshape(2, 8, 4, 2, 2), CTX + ("tp",))
    placed = (
        P("tp", CTX, None),
        P("tp", None, None, None),
        P("tp", None, None),
        P("tp", None, None, None),
        P("tp", None, None),
        P(),
        P(),
        P(),
        P(None, CTX, "tp"),
    )
    return jax.shard_map(
        on_device,
        mesh=fine,
        in_specs=placed,
        out_specs=(P(CTX, "tp"), P(CTX, "tp")),
        check_vma=False,
    )
```

```python
import functools

import jax
import jax.numpy as jnp
from jax import lax
from jax.experimental import pallas as pl
from jax.experimental.pallas import tpu as pltpu
from jax.sharding import Mesh, PartitionSpec as P

HD = 128
BLOCK = 256
D = 4096
CH = 512
CTX = ("yl", "z", "x", "c")
SWAP = [(0, 1), (1, 0)]
BF = jnp.bfloat16
F32 = jnp.float32
LOG2E = 1.4426950408889634
NO_COST = pl.CostEstimate(flops=0, bytes_accessed=0, transcendentals=0)


def elu(v):
    return jnp.where(v > 0, v, jnp.exp(jnp.minimum(v, 0.0)) - 1.0)


def dot(a, b):
    return jnp.dot(a, b, preferred_element_type=F32)


def in_vmem(n):
    return [pl.BlockSpec(memory_space=pltpu.VMEM)] * n


def params(mib):
    return pltpu.CompilerParams(vmem_limit_bytes=mib * 1024 * 1024)


def encoder_kernel(halo_ref, audio_ref, taps_ref, back_ref, down_ref, out_ref, u_ref, e_ref):
    u_ref[0:8, :] = jnp.zeros((8, CH), F32)
    u_ref[8:16, :] = elu(halo_ref[...].astype(F32))
    u_ref[16:, :] = elu(audio_ref[...].astype(F32))
    rows = audio_ref.shape[0] + 8
    inner = dot(u_ref[2 : 2 + rows, :].astype(BF), taps_ref[0])
    inner += dot(u_ref[5 : 5 + rows, :].astype(BF), taps_ref[1])
    inner += dot(u_ref[8 : 8 + rows, :].astype(BF), taps_ref[2])
    hidden = elu(inner).astype(BF)
    branch = dot(hidden, back_ref[...])
    first = (halo_ref[...].astype(F32) + branch[0:8]).astype(BF)
    first = elu(first.astype(F32)).astype(BF).astype(F32)
    rest = (audio_ref[...].astype(F32) + branch[8:]).astype(BF)
    rest = elu(rest.astype(F32)).astype(BF).astype(F32)
    for j in range(CH // 128):
        e_ref[j, 0:8, :] = first[:, j * 128 : (j + 1) * 128]
        e_ref[j, 8:, :] = rest[:, j * 128 : (j + 1) * 128]
    acc = jnp.zeros((BLOCK, CH), F32)
    for k in range(4):
        e = [e_ref[j, pl.ds(6 + k, BLOCK, stride=2), :].astype(BF) for j in range(CH // 128)]
        acc += dot(jnp.concatenate(e, axis=1), down_ref[k])
    out_ref[...] = acc.astype(BF)


def encoder(halo, audio, taps, back, down):
    return pl.pallas_call(
        encoder_kernel,
        in_specs=in_vmem(5),
        out_specs=pl.BlockSpec(memory_space=pltpu.VMEM),
        out_shape=jax.ShapeDtypeStruct((BLOCK, CH), BF),
        scratch_shapes=[pltpu.VMEM((528, CH), F32), pltpu.VMEM((CH // 128, 520, 128), F32)],
        compiler_params=params(20),
        cost_estimate=NO_COST,
    )(halo, audio, taps, back, down)


def swap(a, axis):
    return lax.ppermute(a, axis, SWAP)


def shift(a, by):
    return lax.ppermute(a, "x", [(i, (i + by) % 4) for i in range(4)])


def split_kernel(at_ref, w_ref, near_ref, far_ref, *outs):
    x = at_ref[3]
    for dx in range(4):
        lanes = pl.ds(pl.multiple_of(lax.rem(x + dx, 4) * 256, 256), 256)
        outs[dx][...] = w_ref[:, :, lanes]
    outs[4][0] = near_ref[...]
    outs[4][1] = far_ref[...]


def split(at, w, embed):
    whole = lambda shape: pl.BlockSpec(shape, lambda i, at: (0,) * len(shape))
    return pl.pallas_call(
        split_kernel,
        grid_spec=pltpu.PrefetchScalarGridSpec(
            num_scalar_prefetch=1,
            grid=(1,),
            in_specs=[
                whole((3, 32, 1024)),
                pl.BlockSpec((128, 256), lambda i, at: (at[2], at[0])),
                pl.BlockSpec((128, 256), lambda i, at: (at[2], at[1])),
            ],
            out_specs=[whole((3, 32, 256))] * 4 + [whole((2, 128, 256))],
        ),
        out_shape=[jax.ShapeDtypeStruct((3, 32, 256), BF)] * 4 + [jax.ShapeDtypeStruct((2, 128, 256), BF)],
    )(at, w, embed, embed)


def unused(after):
    return in_vmem(len(after))


def stack_kernel(n, *refs):
    for i in range(n):
        refs[-1][i] = refs[i][...]


def stack(parts, after=()):
    return pl.pallas_call(
        functools.partial(stack_kernel, len(parts)),
        in_specs=in_vmem(len(parts)) + unused(after),
        out_specs=pl.BlockSpec(memory_space=pltpu.VMEM),
        out_shape=jax.ShapeDtypeStruct((len(parts),) + parts[0].shape, parts[0].dtype),
        compiler_params=params(4),
        cost_estimate=NO_COST,
    )(*parts, *after)


def partial_kernel(at_ref, w00, w01, w10, w11, mine_ref, rest_ref, g0, g1, t0, t1, *refs):
    out_ref, w_ref = refs[-2:]
    x, core = at_ref[3], at_ref[4]
    for y, pair in enumerate(((w00, w01), (w10, w11))):
        for c, ref in enumerate(pair):
            for dx in range(4):
                row = lax.rem(x + 4 - dx, 4) * 64 + (core ^ c) * 32
                for j in range(3):
                    w_ref[y, pl.ds(pl.multiple_of(row, 32), 32), j * 256 : (j + 1) * 256] = ref[dx, j]
    part = None
    line = None
    for y, (gain_ref, table_ref) in enumerate(((g0, t0), (g1, t1))):
        w = w_ref[y]
        gain = gain_ref[...]
        embed = jnp.concatenate([mine_ref[y], rest_ref[y]], axis=0).astype(F32) * gain
        table = jnp.concatenate([table_ref[...], jnp.zeros((6, 256), F32)], axis=0) * gain
        high = table.astype(BF)
        low = (table - high.astype(F32)).astype(BF)
        a = dot(embed.astype(BF), w)
        b = dot(high, w) + dot(low, w)
        part = a if part is None else part + a
        line = b if line is None else line + b
    top = line.astype(BF).astype(F32)
    rem = line - top
    rows = [v[s : s + 1, k * 128 : (k + 1) * 128] for v in (top, rem) for s in range(2) for k in range(6)]
    tail = jnp.concatenate(rows + [jnp.zeros((8, 128), F32)], axis=0).astype(BF)
    for i in range(8):
        out_ref[i, :, 0:768] = part[i * 32 : (i + 1) * 32].astype(BF)
        out_ref[i, :, 768:896] = tail


def partial_weights(at, ws, mine, rest, gain, table, after):
    whole = lambda shape: pl.BlockSpec(shape, lambda i, at: (0,) * len(shape))
    here = lambda rows, k: pl.BlockSpec((rows, 256), lambda i, at: (0, at[k]))
    return pl.pallas_call(
        partial_kernel,
        grid_spec=pltpu.PrefetchScalarGridSpec(
            num_scalar_prefetch=1,
            grid=(1,),
            in_specs=[whole((4, 3, 32, 256))] * 4
            + [whole((2, 128, 256))] * 2
            + [here(1, 0), here(1, 1), here(2, 0), here(2, 1)]
            + unused(after),
            out_specs=whole((8, 32, 896)),
            scratch_shapes=[pltpu.VMEM((2, 256, 768), BF)],
        ),
        out_shape=jax.ShapeDtypeStruct((8, 32, 896), BF),
        compiler_params=params(16),
        cost_estimate=NO_COST,
    )(at, *ws, mine, rest, gain, gain, table, table, *after)


def sum_kernel(p_ref, *refs):
    m_ref, line_ref = refs[-2:]
    total = jnp.sum(p_ref[...].astype(F32), axis=0)
    m = total[:, :768].astype(BF)
    for i in range(8):
        m_ref[i] = m
    both = total[0:12, 768:] + total[12:24, 768:]
    line_ref[...] = jnp.zeros((8, 768), F32)
    for s in range(2):
        for k in range(6):
            line_ref[s : s + 1, k * 128 : (k + 1) * 128] = both[s * 6 + k : s * 6 + k + 1]


def sum_weights(packed, after):
    return pl.pallas_call(
        sum_kernel,
        in_specs=in_vmem(1) + unused(after),
        out_specs=in_vmem(2),
        out_shape=[jax.ShapeDtypeStruct((8, 32, 768), BF), jax.ShapeDtypeStruct((8, 768), F32)],
        compiler_params=params(8),
        cost_estimate=NO_COST,
    )(packed, *after)


def term_kernel(at_ref, latent_ref, embed_ref, *refs):
    give_ref, own_ref = refs[-2:]
    term = dot(latent_ref[...], embed_ref[...])
    mine = at_ref[5] == pl.program_id(0) // 2

    @pl.when(mine)
    def _():
        own_ref[...] = term.astype(BF)

    @pl.when(jnp.logical_not(mine))
    def _():
        give_ref[...] = term.astype(BF)


def terms(at, latent, embed, after):
    def give_at(i, at):
        return (0, jnp.where(at[5] == 0, jnp.maximum(i - 2, 0), jnp.minimum(i, 1)))

    def own_at(i, at):
        return (0, jnp.where(at[5] == 1, jnp.maximum(i - 2, 0), jnp.minimum(i, 1)))

    return pl.pallas_call(
        term_kernel,
        grid_spec=pltpu.PrefetchScalarGridSpec(
            num_scalar_prefetch=1,
            grid=(4,),
            in_specs=[pl.BlockSpec((BLOCK, CH), lambda i, at: (0, 0)), pl.BlockSpec((CH, 1024), lambda i, at: (0, i))]
            + unused(after),
            out_specs=[pl.BlockSpec((BLOCK, 1024), give_at), pl.BlockSpec((BLOCK, 1024), own_at)],
        ),
        out_shape=[jax.ShapeDtypeStruct((BLOCK, D // 2), BF)] * 2,
        compiler_params=params(16),
        cost_estimate=NO_COST,
    )(at, latent, embed, *after)


def embed_kernel(at_ref, own_ref, got_ref, active_ref, table_ref, *refs):
    out_ref, square_ref = refs[-2:]
    act = active_ref[:, pl.ds(at_ref[3] + 4, 1), :].reshape(2, BLOCK)
    cols = jnp.concatenate([act, jnp.zeros((6, BLOCK), F32)], axis=0).T
    x = own_ref[...].astype(F32) + got_ref[...].astype(F32)
    x = x + cols[:, 0:1] * table_ref[0:1] + cols[:, 1:2] * table_ref[1:2]
    out_ref[...] = x.astype(BF)
    square = jnp.sum(x * x, axis=1, keepdims=True)
    square = jnp.broadcast_to(square, (BLOCK, 128)).T[0:8]

    @pl.when(pl.program_id(0) == 0)
    def _():
        square_ref[...] = square

    @pl.when(pl.program_id(0) != 0)
    def _():
        square_ref[...] += square


def embed_rows(at, own, got, active, table, after):
    tile = pl.BlockSpec((BLOCK, 1024), lambda i, at: (0, i))
    return pl.pallas_call(
        embed_kernel,
        grid_spec=pltpu.PrefetchScalarGridSpec(
            num_scalar_prefetch=1,
            grid=(2,),
            in_specs=[
                tile,
                tile,
                pl.BlockSpec((2, 8, BLOCK), lambda i, at: (0, 0, 0)),
                pl.BlockSpec((2, 1024), lambda i, at: (0, at[5] * 2 + i)),
            ]
            + unused(after),
            out_specs=[tile, pl.BlockSpec((8, BLOCK), lambda i, at: (0, 0))],
        ),
        out_shape=[jax.ShapeDtypeStruct((BLOCK, D // 2), BF), jax.ShapeDtypeStruct((8, BLOCK), F32)],
        compiler_params=params(16),
        cost_estimate=pl.CostEstimate(flops=20000000000, bytes_accessed=0, transcendentals=0),
    )(at, own, got, active, table, *after)


def project_rows(row, blocks, m_ref, line_ref, active_ref, scale_ref, at_ref, kv_ref, q_ref):
    x = at_ref[3]
    cols = slice(0, 768) if q_ref is not None else slice(256, 768)
    w0, w1 = m_ref[0:512, cols], m_ref[512:1024, cols]
    line = line_ref[:, cols]
    for dx in range(4):
        at = lax.rem(x + dx, 4)
        act = active_ref[:, pl.ds(4 * row + at, 1), :].reshape(2, BLOCK)
        side = jnp.concatenate([act, scale_ref[pl.ds(at ^ x, 1), :], jnp.zeros((5, BLOCK), F32)], axis=0).T
        acc = dot(blocks[dx][0], w0) + dot(blocks[dx][1], w1)
        acc = (acc + side[:, 0:1] * line[0:1] + side[:, 1:2] * line[1:2]) * side[:, 2:3]
        kv_ref[at] = acc[:, -512:].astype(BF)
        if q_ref is not None:
            q_ref[at] = (acc[:, :256] * (HD**-0.5 * LOG2E)).astype(BF)


def project_own_kernel(at_ref, a, al, ar, af, m00, m01, m10, m11, line_ref, active_ref, scale_ref, kv_ref, q_ref, m_ref):
    core, yl = at_ref[4], at_ref[6]
    for y, pair in enumerate(((m00, m01), (m10, m11))):
        for c, ref in enumerate(pair):
            row = ((yl ^ y) * 2 + (core ^ c)) * 128
            for s in range(2):
                m_ref[pl.ds(pl.multiple_of(s * 512 + row, 128), 128), :] = ref[s * 128 : (s + 1) * 128, :]
    project_rows(1, (a, ar, af, al), m_ref, line_ref, active_ref, scale_ref, at_ref, kv_ref, q_ref)


def project_prev_kernel(at_ref, b, bl, br, bf, m_ref, line_ref, active_ref, scale_ref, kv_ref):
    project_rows(0, (b, br, bf, bl), m_ref, line_ref, active_ref, scale_ref, at_ref, kv_ref, None)


def project(kernel, outs, *args):
    return pl.pallas_call(
        kernel,
        in_specs=[pl.BlockSpec(memory_space=pltpu.SMEM)] + in_vmem(len(args) - 1),
        out_specs=in_vmem(len(outs)),
        out_shape=outs,
        compiler_params=params(10),
        cost_estimate=NO_COST,
    )(*args)


def attention_kernel(n, place_ref, q_ref, om_ref, ot_ref, pm_ref, pt_ref, *o_refs):
    x, core, first = place_ref[0], place_ref[1], place_ref[2]
    half = BLOCK // 2
    cols = lax.broadcasted_iota(jnp.int32, (half, BLOCK), 1)
    ones = jnp.ones((8 * BLOCK, HD), BF)
    contract = (((1,), (1,)), ((), ()))
    for step in range(n):
        at = lax.rem(x + place_ref[3 + step], 4)
        blocks, penalties = [], []
        for own_ref, prev_ref, begin in ((om_ref, pm_ref, at + 1), (ot_ref, pt_ref, at + core)):
            for j in range(4):
                m = begin + j
                i = lax.rem(m, 4)
                blocks.append(jnp.where(m >= 4, own_ref[i], prev_ref[i]))
                penalties.append(jnp.where((m < 4) & (first == 1), 1e30, 0.0))
        kv = jnp.concatenate(blocks, axis=0)
        for h in range(2):
            q = q_ref[at, :, h * HD : (h + 1) * HD]
            k = kv[:, h * HD : (h + 1) * HD]
            v = jnp.concatenate([kv[:, 256 + h * HD : 256 + (h + 1) * HD], ones], axis=1)
            for begin in (0, half):
                rows = lax.broadcasted_iota(jnp.int32, (half, BLOCK), 0) + begin
                s = lax.dot_general(q[begin : begin + half], k, contract, preferred_element_type=F32)
                s = [s[:, j * BLOCK : (j + 1) * BLOCK] for j in range(8)]
                s[3] = jnp.where(cols <= rows, s[3], -1e30)
                s[4] = jnp.where(cols > rows, s[4], -1e30)
                tops = [jnp.max(v, axis=1, keepdims=True) - penalty for v, penalty in zip(s, penalties)]
                top = functools.reduce(jnp.maximum, tops)
                p = [jnp.exp2(v - (top + penalty)).astype(BF) for v, penalty in zip(s, penalties)]
                o = dot(jnp.concatenate(p, axis=1), v)
                o_refs[step][begin : begin + half, h * HD : (h + 1) * HD] = (o[:, :HD] / o[:, HD:]).astype(BF)


def attention(place, offsets, *args):
    n = len(offsets)
    return pl.pallas_call(
        functools.partial(attention_kernel, n),
        in_specs=[pl.BlockSpec(memory_space=pltpu.SMEM)] + in_vmem(5),
        out_specs=in_vmem(n),
        out_shape=[jax.ShapeDtypeStruct((BLOCK, 256), BF)] * n,
        compiler_params=params(16),
        cost_estimate=NO_COST,
    )(jnp.concatenate([place, jnp.array(offsets, jnp.int32)]), *args)


def collect_kernel(place_ref, a_ref, b_ref, c_ref, d_ref, o_ref):
    for dx, ref in enumerate((a_ref, b_ref, c_ref, d_ref)):
        at = lax.rem(place_ref[0] + 4 - dx, 4)
        o_ref[:, pl.ds(pl.multiple_of(at * 256, 256), 256)] = ref[...]


def collect(place, parts):
    return pl.pallas_call(
        collect_kernel,
        in_specs=[pl.BlockSpec(memory_space=pltpu.SMEM)] + in_vmem(4),
        out_specs=pl.BlockSpec(memory_space=pltpu.VMEM),
        out_shape=jax.ShapeDtypeStruct((BLOCK, 1024), BF),
        compiler_params=params(20),
    )(place, *parts)


def on_device(
    audio_feats,
    res_conv,
    res_out,
    down_conv,
    stream_embed,
    turn_lengths,
    speaker_table,
    norm_gain,
    qkv_weight,
):
    tp = lax.axis_index("tp")
    x_at = lax.axis_index("x")
    core = lax.axis_index("c")
    yl = lax.axis_index("yl")
    z = lax.axis_index("z")
    row = yl * 8 + z
    at = jnp.stack([yl * 8 + z, (1 - yl) * 8 + z, yl * 2 + core, x_at, core, tp, yl]).astype(jnp.int32)
    behind = [(i, i + 1) for i in range(15)]

    audio = audio_feats[0]
    halo = lax.ppermute(audio[-8:], CTX, [(i, i + 1) for i in range(127)])
    embed = stream_embed[0]
    *chunks, mine = split(at, qkv_weight, embed)
    arrived = [shift(chunks[dx], dx) for dx in (1, 2, 3)]
    rest = swap(mine, "tp")

    latent = encoder(halo, audio, res_conv[0], res_out[0], down_conv[0])
    give, own = terms(at, latent, embed, ())
    other = swap(latent, "tp")
    a = stack([latent, other])
    prev = lax.ppermute(latent, ("yl", "z"), behind)
    b = stack([prev, lax.ppermute(other, ("yl", "z"), behind)])
    al, ar = shift(a, 1), shift(a, 3)
    bl, br = shift(b, 1), shift(b, 3)
    af, bf = shift(al, 1), shift(br, 3)

    w00 = stack([chunks[0]] + arrived, (latent, rest))
    w10 = swap(w00, "yl")
    w01 = swap(w00, "c")
    w11 = swap(w10, "c")
    packed = partial_weights(at, (w00, w01, w10, w11), mine, rest, norm_gain[None], speaker_table, (give, a, prev))
    packed = lax.all_to_all(packed, "z", 0, 0, tiled=True)
    m, lines = sum_weights(packed, ())
    bounds = jnp.cumsum(turn_lengths, axis=1)
    start = ((row - 1 + jnp.arange(2)[:, None]) * 8 + 2 * jnp.arange(4)[None, :] + core) * BLOCK
    frames = start.reshape(8, 1) + jnp.arange(BLOCK)
    turn = jnp.sum((bounds[:, :, None, None] <= frames[None, None]).astype(jnp.int32), axis=1)
    active = (turn % 2 == 1).astype(F32)

    got = swap(give, "tp")
    embedded, square = embed_rows(at, own, got, active, speaker_table, (al, ar, b))
    square = square[0:1]
    beside = lax.ppermute(square, "x", [(i, i ^ 1) for i in range(4)])
    across = lax.ppermute(square, ("x", "tp"), [(i, i ^ 3) for i in range(8)])
    square = jnp.concatenate([square + swap(square, "tp"), beside + across])
    scale = lax.rsqrt(square * (1.0 / D) + 1e-05)
    scales = jnp.concatenate([scale, lax.ppermute(scale, "x", [(i, i ^ 2) for i in range(4)])])
    m00 = lax.all_to_all(m, "z", 0, 0, tiled=True).reshape(256, 768)
    (m00,) = stack([m00], (scales, bl, br))
    m10 = swap(m00, "yl")
    m01 = swap(m00, "c")
    m11 = swap(m10, "c")
    scales_prev = lax.ppermute(scales, ("yl", "z"), behind)

    kv = jax.ShapeDtypeStruct((4, BLOCK, 512), BF)
    half = jax.ShapeDtypeStruct((4, BLOCK, 256), BF)
    full = jax.ShapeDtypeStruct((1024, 768), BF)
    om, q, whole = project(
        project_own_kernel, (kv, half, full), at, a, al, ar, af, m00, m01, m10, m11, lines, active, scales
    )
    ot = swap(om, "c")
    (pm,) = project(project_prev_kernel, (kv,), at, b, bl, br, bf, whole, lines, active, scales_prev)
    pt = swap(pm, "c")

    place = jnp.stack([x_at, core, (row == 0).astype(jnp.int32)]).astype(jnp.int32)
    blocks = (q, om, ot, pm, pt)
    sent = (2, 1, 3)
    parts = dict(zip(sent, attention(place, sent, *blocks)))
    parts = {dx: shift(part, dx) for dx, part in parts.items()}
    (parts[0],) = attention(place, (0,), *blocks)
    return embedded, collect(place, [parts[dx] for dx in range(4)])


def solution(mesh):
    fine = Mesh(mesh.devices.reshape(2, 8, 4, 2, 2), CTX + ("tp",))
    placed = (
        P("tp", CTX, None),
        P("tp", None, None, None),
        P("tp", None, None),
        P("tp", None, None, None),
        P("tp", None, None),
        P(),
        P(),
        P(),
        P(None, CTX, "tp"),
    )
    return jax.shard_map(
        on_device,
        mesh=fine,
        in_specs=placed,
        out_specs=(P(CTX, "tp"), P(CTX, "tp")),
        check_vma=False,
    )
```

```python
import functools

import jax
import jax.numpy as jnp
from jax import lax
from jax.experimental import pallas as pl
from jax.experimental.pallas import tpu as pltpu
from jax.sharding import Mesh, PartitionSpec as P

HD = 128
BLOCK = 256
D = 4096
CH = 512
CTX = ("yl", "z", "x", "c")
SWAP = [(0, 1), (1, 0)]
BF = jnp.bfloat16
F32 = jnp.float32
LOG2E = 1.4426950408889634
NO_COST = pl.CostEstimate(flops=0, bytes_accessed=0, transcendentals=0)


def elu(v):
    return jnp.where(v > 0, v, jnp.exp(jnp.minimum(v, 0.0)) - 1.0)


def dot(a, b):
    return jnp.dot(a, b, preferred_element_type=F32)


def in_vmem(n):
    return [pl.BlockSpec(memory_space=pltpu.VMEM)] * n


def params(mib):
    return pltpu.CompilerParams(vmem_limit_bytes=mib * 1024 * 1024)


def encoder_kernel(halo_ref, audio_ref, taps_ref, back_ref, down_ref, out_ref, u_ref, e_ref):
    u_ref[0:8, :] = jnp.zeros((8, CH), F32)
    u_ref[8:16, :] = elu(halo_ref[...].astype(F32))
    u_ref[16:, :] = elu(audio_ref[...].astype(F32))
    rows = audio_ref.shape[0] + 8
    inner = dot(u_ref[2 : 2 + rows, :].astype(BF), taps_ref[0])
    inner += dot(u_ref[5 : 5 + rows, :].astype(BF), taps_ref[1])
    inner += dot(u_ref[8 : 8 + rows, :].astype(BF), taps_ref[2])
    hidden = elu(inner).astype(BF)
    branch = dot(hidden, back_ref[...])
    first = (halo_ref[...].astype(F32) + branch[0:8]).astype(BF)
    first = elu(first.astype(F32)).astype(BF).astype(F32)
    rest = (audio_ref[...].astype(F32) + branch[8:]).astype(BF)
    rest = elu(rest.astype(F32)).astype(BF).astype(F32)
    for j in range(CH // 128):
        e_ref[j, 0:8, :] = first[:, j * 128 : (j + 1) * 128]
        e_ref[j, 8:, :] = rest[:, j * 128 : (j + 1) * 128]
    acc = jnp.zeros((BLOCK, CH), F32)
    for k in range(4):
        e = [e_ref[j, pl.ds(6 + k, BLOCK, stride=2), :].astype(BF) for j in range(CH // 128)]
        acc += dot(jnp.concatenate(e, axis=1), down_ref[k])
    out_ref[...] = acc.astype(BF)


def encoder(halo, audio, taps, back, down):
    return pl.pallas_call(
        encoder_kernel,
        in_specs=in_vmem(5),
        out_specs=pl.BlockSpec(memory_space=pltpu.VMEM),
        out_shape=jax.ShapeDtypeStruct((BLOCK, CH), BF),
        scratch_shapes=[pltpu.VMEM((528, CH), F32), pltpu.VMEM((CH // 128, 520, 128), F32)],
        compiler_params=params(20),
        cost_estimate=NO_COST,
    )(halo, audio, taps, back, down)


def swap(a, axis):
    return lax.ppermute(a, axis, SWAP)


def shift(a, by):
    return lax.ppermute(a, "x", [(i, (i + by) % 4) for i in range(4)])


def split_kernel(at_ref, w_ref, near_ref, far_ref, *outs):
    x = at_ref[3]
    for dx in range(4):
        lanes = pl.ds(pl.multiple_of(lax.rem(x + dx, 4) * 256, 256), 256)
        outs[dx][...] = w_ref[:, :, lanes]
    outs[4][0] = near_ref[...]
    outs[4][1] = far_ref[...]


def split(at, w, embed):
    whole = lambda shape: pl.BlockSpec(shape, lambda i, at: (0,) * len(shape))
    return pl.pallas_call(
        split_kernel,
        grid_spec=pltpu.PrefetchScalarGridSpec(
            num_scalar_prefetch=1,
            grid=(1,),
            in_specs=[
                whole((3, 32, 1024)),
                pl.BlockSpec((128, 256), lambda i, at: (at[2], at[0])),
                pl.BlockSpec((128, 256), lambda i, at: (at[2], at[1])),
            ],
            out_specs=[whole((3, 32, 256))] * 4 + [whole((2, 128, 256))],
        ),
        out_shape=[jax.ShapeDtypeStruct((3, 32, 256), BF)] * 4 + [jax.ShapeDtypeStruct((2, 128, 256), BF)],
    )(at, w, embed, embed)


def unused(after):
    return in_vmem(len(after))


def stack_kernel(n, *refs):
    for i in range(n):
        refs[-1][i] = refs[i][...]


def stack(parts, after=()):
    return pl.pallas_call(
        functools.partial(stack_kernel, len(parts)),
        in_specs=in_vmem(len(parts)) + unused(after),
        out_specs=pl.BlockSpec(memory_space=pltpu.VMEM),
        out_shape=jax.ShapeDtypeStruct((len(parts),) + parts[0].shape, parts[0].dtype),
        compiler_params=params(4),
        cost_estimate=NO_COST,
    )(*parts, *after)


def partial_kernel(at_ref, w00, w01, w10, w11, mine_ref, rest_ref, g0, g1, t0, t1, *refs):
    out_ref, w_ref = refs[-2:]
    x, core = at_ref[3], at_ref[4]
    for y, pair in enumerate(((w00, w01), (w10, w11))):
        for c, ref in enumerate(pair):
            for dx in range(4):
                row = lax.rem(x + 4 - dx, 4) * 64 + (core ^ c) * 32
                for j in range(3):
                    w_ref[y, pl.ds(pl.multiple_of(row, 32), 32), j * 256 : (j + 1) * 256] = ref[dx, j]
    part = None
    line = None
    for y, (gain_ref, table_ref) in enumerate(((g0, t0), (g1, t1))):
        w = w_ref[y]
        gain = gain_ref[...]
        embed = jnp.concatenate([mine_ref[y], rest_ref[y]], axis=0).astype(F32) * gain
        table = jnp.concatenate([table_ref[...], jnp.zeros((6, 256), F32)], axis=0) * gain
        high = table.astype(BF)
        low = (table - high.astype(F32)).astype(BF)
        a = dot(embed.astype(BF), w)
        b = dot(high, w) + dot(low, w)
        part = a if part is None else part + a
        line = b if line is None else line + b
    top = line.astype(BF).astype(F32)
    rem = line - top
    rows = [v[s : s + 1, k * 128 : (k + 1) * 128] for v in (top, rem) for s in range(2) for k in range(6)]
    tail = jnp.concatenate(rows + [jnp.zeros((8, 128), F32)], axis=0).astype(BF)
    for i in range(8):
        out_ref[i, :, 0:768] = part[i * 32 : (i + 1) * 32].astype(BF)
        out_ref[i, :, 768:896] = tail


def partial_weights(at, ws, mine, rest, gain, table, after):
    whole = lambda shape: pl.BlockSpec(shape, lambda i, at: (0,) * len(shape))
    here = lambda rows, k: pl.BlockSpec((rows, 256), lambda i, at: (0, at[k]))
    return pl.pallas_call(
        partial_kernel,
        grid_spec=pltpu.PrefetchScalarGridSpec(
            num_scalar_prefetch=1,
            grid=(1,),
            in_specs=[whole((4, 3, 32, 256))] * 4
            + [whole((2, 128, 256))] * 2
            + [here(1, 0), here(1, 1), here(2, 0), here(2, 1)]
            + unused(after),
            out_specs=whole((8, 32, 896)),
            scratch_shapes=[pltpu.VMEM((2, 256, 768), BF)],
        ),
        out_shape=jax.ShapeDtypeStruct((8, 32, 896), BF),
        compiler_params=params(16),
        cost_estimate=NO_COST,
    )(at, *ws, mine, rest, gain, gain, table, table, *after)


def sum_kernel(p_ref, *refs):
    m_ref, line_ref = refs[-2:]
    total = jnp.sum(p_ref[...].astype(F32), axis=0)
    m = total[:, :768].astype(BF)
    for i in range(8):
        m_ref[i] = m
    both = total[0:12, 768:] + total[12:24, 768:]
    line_ref[...] = jnp.zeros((8, 768), F32)
    for s in range(2):
        for k in range(6):
            line_ref[s : s + 1, k * 128 : (k + 1) * 128] = both[s * 6 + k : s * 6 + k + 1]


def sum_weights(packed, after):
    return pl.pallas_call(
        sum_kernel,
        in_specs=in_vmem(1) + unused(after),
        out_specs=in_vmem(2),
        out_shape=[jax.ShapeDtypeStruct((8, 32, 768), BF), jax.ShapeDtypeStruct((8, 768), F32)],
        compiler_params=params(8),
        cost_estimate=NO_COST,
    )(packed, *after)


def term_kernel(at_ref, latent_ref, embed_ref, *refs):
    give_ref, own_ref = refs[-2:]
    term = dot(latent_ref[...], embed_ref[...])
    mine = at_ref[5] == pl.program_id(0) // 2

    @pl.when(mine)
    def _():
        own_ref[...] = term.astype(BF)

    @pl.when(jnp.logical_not(mine))
    def _():
        give_ref[...] = term.astype(BF)


def terms(at, latent, embed, after):
    def give_at(i, at):
        return (0, jnp.where(at[5] == 0, jnp.maximum(i - 2, 0), jnp.minimum(i, 1)))

    def own_at(i, at):
        return (0, jnp.where(at[5] == 1, jnp.maximum(i - 2, 0), jnp.minimum(i, 1)))

    return pl.pallas_call(
        term_kernel,
        grid_spec=pltpu.PrefetchScalarGridSpec(
            num_scalar_prefetch=1,
            grid=(4,),
            in_specs=[pl.BlockSpec((BLOCK, CH), lambda i, at: (0, 0)), pl.BlockSpec((CH, 1024), lambda i, at: (0, i))]
            + unused(after),
            out_specs=[pl.BlockSpec((BLOCK, 1024), give_at), pl.BlockSpec((BLOCK, 1024), own_at)],
        ),
        out_shape=[jax.ShapeDtypeStruct((BLOCK, D // 2), BF)] * 2,
        compiler_params=params(16),
        cost_estimate=NO_COST,
    )(at, latent, embed, *after)


def embed_kernel(at_ref, own_ref, got_ref, active_ref, table_ref, *refs):
    out_ref, square_ref = refs[-2:]
    act = active_ref[:, pl.ds(at_ref[3] + 4, 1), :].reshape(2, BLOCK)
    cols = jnp.concatenate([act, jnp.zeros((6, BLOCK), F32)], axis=0).T
    x = own_ref[...].astype(F32) + got_ref[...].astype(F32)
    x = x + cols[:, 0:1] * table_ref[0:1] + cols[:, 1:2] * table_ref[1:2]
    out_ref[...] = x.astype(BF)
    square = jnp.sum(x * x, axis=1, keepdims=True)
    square = jnp.broadcast_to(square, (BLOCK, 128)).T[0:8]

    @pl.when(pl.program_id(0) == 0)
    def _():
        square_ref[...] = square

    @pl.when(pl.program_id(0) != 0)
    def _():
        square_ref[...] += square


def embed_rows(at, own, got, active, table, after):
    tile = pl.BlockSpec((BLOCK, 1024), lambda i, at: (0, i))
    return pl.pallas_call(
        embed_kernel,
        grid_spec=pltpu.PrefetchScalarGridSpec(
            num_scalar_prefetch=1,
            grid=(2,),
            in_specs=[
                tile,
                tile,
                pl.BlockSpec((2, 8, BLOCK), lambda i, at: (0, 0, 0)),
                pl.BlockSpec((2, 1024), lambda i, at: (0, at[5] * 2 + i)),
            ]
            + unused(after),
            out_specs=[tile, pl.BlockSpec((8, BLOCK), lambda i, at: (0, 0))],
        ),
        out_shape=[jax.ShapeDtypeStruct((BLOCK, D // 2), BF), jax.ShapeDtypeStruct((8, BLOCK), F32)],
        compiler_params=params(16),
        cost_estimate=pl.CostEstimate(flops=20000000000, bytes_accessed=0, transcendentals=0),
    )(at, own, got, active, table, *after)


def project_rows(row, blocks, m_ref, line_ref, active_ref, scale_ref, at_ref, kv_ref, q_ref):
    x = at_ref[3]
    cols = slice(0, 768) if q_ref is not None else slice(256, 768)
    w0, w1 = m_ref[0:512, cols], m_ref[512:1024, cols]
    line = line_ref[:, cols]
    for dx in range(4):
        at = lax.rem(x + dx, 4)
        act = active_ref[:, pl.ds(4 * row + at, 1), :].reshape(2, BLOCK)
        side = jnp.concatenate([act, scale_ref[pl.ds(at ^ x, 1), :], jnp.zeros((5, BLOCK), F32)], axis=0).T
        acc = dot(blocks[dx][0], w0) + dot(blocks[dx][1], w1)
        acc = (acc + side[:, 0:1] * line[0:1] + side[:, 1:2] * line[1:2]) * side[:, 2:3]
        kv_ref[at] = acc[:, -512:].astype(BF)
        if q_ref is not None:
            q_ref[at] = (acc[:, :256] * (HD**-0.5 * LOG2E)).astype(BF)


def project_own_kernel(at_ref, a, al, ar, af, m00, m01, m10, m11, line_ref, active_ref, scale_ref, kv_ref, q_ref, m_ref):
    core, yl = at_ref[4], at_ref[6]
    for y, pair in enumerate(((m00, m01), (m10, m11))):
        for c, ref in enumerate(pair):
            row = ((yl ^ y) * 2 + (core ^ c)) * 128
            for s in range(2):
                m_ref[pl.ds(pl.multiple_of(s * 512 + row, 128), 128), :] = ref[s * 128 : (s + 1) * 128, :]
    project_rows(1, (a, ar, af, al), m_ref, line_ref, active_ref, scale_ref, at_ref, kv_ref, q_ref)


def project_prev_kernel(at_ref, b, bl, br, bf, m_ref, line_ref, active_ref, scale_ref, kv_ref):
    project_rows(0, (b, br, bf, bl), m_ref, line_ref, active_ref, scale_ref, at_ref, kv_ref, None)


def project(kernel, outs, *args):
    return pl.pallas_call(
        kernel,
        in_specs=[pl.BlockSpec(memory_space=pltpu.SMEM)] + in_vmem(len(args) - 1),
        out_specs=in_vmem(len(outs)),
        out_shape=outs,
        compiler_params=params(10),
        cost_estimate=NO_COST,
    )(*args)


def attention_kernel(n, place_ref, q_ref, om_ref, ot_ref, pm_ref, pt_ref, *o_refs):
    x, core, first = place_ref[0], place_ref[1], place_ref[2]
    half = BLOCK // 2
    cols = lax.broadcasted_iota(jnp.int32, (half, BLOCK), 1)
    ones = jnp.ones((8 * BLOCK, HD), BF)
    contract = (((1,), (1,)), ((), ()))
    for step in range(n):
        at = lax.rem(x + place_ref[3 + step], 4)
        blocks, penalties = [], []
        for own_ref, prev_ref, begin in ((om_ref, pm_ref, at + 1), (ot_ref, pt_ref, at + core)):
            for j in range(4):
                m = begin + j
                i = lax.rem(m, 4)
                blocks.append(jnp.where(m >= 4, own_ref[i], prev_ref[i]))
                penalties.append(jnp.where((m < 4) & (first == 1), 1e30, 0.0))
        kv = jnp.concatenate(blocks, axis=0)
        for h in range(2):
            q = q_ref[at, :, h * HD : (h + 1) * HD]
            k = kv[:, h * HD : (h + 1) * HD]
            v = jnp.concatenate([kv[:, 256 + h * HD : 256 + (h + 1) * HD], ones], axis=1)
            for begin in (0, half):
                rows = lax.broadcasted_iota(jnp.int32, (half, BLOCK), 0) + begin
                s = lax.dot_general(q[begin : begin + half], k, contract, preferred_element_type=F32)
                s = [s[:, j * BLOCK : (j + 1) * BLOCK] for j in range(8)]
                s[3] = jnp.where(cols <= rows, s[3], -1e30)
                s[4] = jnp.where(cols > rows, s[4], -1e30)
                tops = [jnp.max(v, axis=1, keepdims=True) - penalty for v, penalty in zip(s, penalties)]
                top = functools.reduce(jnp.maximum, tops)
                p = [jnp.exp2(v - (top + penalty)).astype(BF) for v, penalty in zip(s, penalties)]
                o = dot(jnp.concatenate(p, axis=1), v)
                o_refs[step][begin : begin + half, h * HD : (h + 1) * HD] = (o[:, :HD] / o[:, HD:]).astype(BF)


def attention(place, offsets, *args):
    n = len(offsets)
    return pl.pallas_call(
        functools.partial(attention_kernel, n),
        in_specs=[pl.BlockSpec(memory_space=pltpu.SMEM)] + in_vmem(5),
        out_specs=in_vmem(n),
        out_shape=[jax.ShapeDtypeStruct((BLOCK, 256), BF)] * n,
        compiler_params=params(16),
        cost_estimate=NO_COST,
    )(jnp.concatenate([place, jnp.array(offsets, jnp.int32)]), *args)


def collect_kernel(place_ref, a_ref, b_ref, c_ref, d_ref, o_ref):
    for dx, ref in enumerate((a_ref, b_ref, c_ref, d_ref)):
        at = lax.rem(place_ref[0] + 4 - dx, 4)
        o_ref[:, pl.ds(pl.multiple_of(at * 256, 256), 256)] = ref[...]


def collect(place, parts):
    return pl.pallas_call(
        collect_kernel,
        in_specs=[pl.BlockSpec(memory_space=pltpu.SMEM)] + in_vmem(4),
        out_specs=pl.BlockSpec(memory_space=pltpu.VMEM),
        out_shape=jax.ShapeDtypeStruct((BLOCK, 1024), BF),
        compiler_params=params(20),
    )(place, *parts)


def on_device(
    audio_feats,
    res_conv,
    res_out,
    down_conv,
    stream_embed,
    turn_lengths,
    speaker_table,
    norm_gain,
    qkv_weight,
):
    tp = lax.axis_index("tp")
    x_at = lax.axis_index("x")
    core = lax.axis_index("c")
    yl = lax.axis_index("yl")
    z = lax.axis_index("z")
    row = yl * 8 + z
    at = jnp.stack([yl * 8 + z, (1 - yl) * 8 + z, yl * 2 + core, x_at, core, tp, yl]).astype(jnp.int32)
    behind = [(i, i + 1) for i in range(15)]

    audio = audio_feats[0]
    halo = lax.ppermute(audio[-8:], CTX, [(i, i + 1) for i in range(127)])
    embed = stream_embed[0]
    *chunks, mine = split(at, qkv_weight, embed)
    arrived = [shift(chunks[dx], dx) for dx in (1, 2, 3)]
    rest = swap(mine, "tp")

    latent = encoder(halo, audio, res_conv[0], res_out[0], down_conv[0])
    give, own = terms(at, latent, embed, ())
    other = swap(latent, "tp")
    a = stack([latent, other])
    prev = lax.ppermute(latent, ("yl", "z"), behind)
    b = stack([prev, lax.ppermute(other, ("yl", "z"), behind)])
    al, ar = shift(a, 1), shift(a, 3)
    bl, br = shift(b, 1), shift(b, 3)
    af, bf = shift(al, 1), shift(br, 3)

    w00 = stack([chunks[0]] + arrived, (latent, rest))
    w10 = swap(w00, "yl")
    w01 = swap(w00, "c")
    w11 = swap(w10, "c")
    packed = partial_weights(at, (w00, w01, w10, w11), mine, rest, norm_gain[None], speaker_table, (give, other, prev))
    packed = lax.all_to_all(packed, "z", 0, 0, tiled=True)
    m, lines = sum_weights(packed, ())
    bounds = jnp.cumsum(turn_lengths, axis=1)
    start = ((row - 1 + jnp.arange(2)[:, None]) * 8 + 2 * jnp.arange(4)[None, :] + core) * BLOCK
    frames = start.reshape(8, 1) + jnp.arange(BLOCK)
    turn = jnp.sum((bounds[:, :, None, None] <= frames[None, None]).astype(jnp.int32), axis=1)
    active = (turn % 2 == 1).astype(F32)

    got = swap(give, "tp")
    embedded, square = embed_rows(at, own, got, active, speaker_table, (al, ar, b))
    square = square[0:1]
    beside = lax.ppermute(square, "x", [(i, i ^ 1) for i in range(4)])
    across = lax.ppermute(square, ("x", "tp"), [(i, i ^ 3) for i in range(8)])
    square = jnp.concatenate([square + swap(square, "tp"), beside + across])
    scale = lax.rsqrt(square * (1.0 / D) + 1e-05)
    scales = jnp.concatenate([scale, lax.ppermute(scale, "x", [(i, i ^ 2) for i in range(4)])])
    m00 = lax.all_to_all(m, "z", 0, 0, tiled=True).reshape(256, 768)
    (m00,) = stack([m00], (scales, bl, br))
    m10 = swap(m00, "yl")
    m01 = swap(m00, "c")
    m11 = swap(m10, "c")
    scales_prev = lax.ppermute(scales, ("yl", "z"), behind)

    kv = jax.ShapeDtypeStruct((4, BLOCK, 512), BF)
    half = jax.ShapeDtypeStruct((4, BLOCK, 256), BF)
    full = jax.ShapeDtypeStruct((1024, 768), BF)
    om, q, whole = project(
        project_own_kernel, (kv, half, full), at, a, al, ar, af, m00, m01, m10, m11, lines, active, scales
    )
    ot = swap(om, "c")
    (pm,) = project(project_prev_kernel, (kv,), at, b, bl, br, bf, whole, lines, active, scales_prev)
    pt = swap(pm, "c")

    place = jnp.stack([x_at, core, (row == 0).astype(jnp.int32)]).astype(jnp.int32)
    blocks = (q, om, ot, pm, pt)
    sent = (2, 1, 3)
    parts = dict(zip(sent, attention(place, sent, *blocks)))
    parts = {dx: shift(part, dx) for dx, part in parts.items()}
    (parts[0],) = attention(place, (0,), *blocks)
    return embedded, collect(place, [parts[dx] for dx in range(4)])


def solution(mesh):
    fine = Mesh(mesh.devices.reshape(2, 8, 4, 2, 2), CTX + ("tp",))
    placed = (
        P("tp", CTX, None),
        P("tp", None, None, None),
        P("tp", None, None),
        P("tp", None, None, None),
        P("tp", None, None),
        P(),
        P(),
        P(),
        P(None, CTX, "tp"),
    )
    return jax.shard_map(
        on_device,
        mesh=fine,
        in_specs=placed,
        out_specs=(P(CTX, "tp"), P(CTX, "tp")),
        check_vma=False,
    )
```

```python
import functools

import jax
import jax.numpy as jnp
from jax import lax
from jax.experimental import pallas as pl
from jax.experimental.pallas import tpu as pltpu
from jax.sharding import Mesh, PartitionSpec as P

HD = 128
BLOCK = 256
D = 4096
CH = 512
CTX = ("yl", "z", "x", "c")
SWAP = [(0, 1), (1, 0)]
BF = jnp.bfloat16
F32 = jnp.float32
LOG2E = 1.4426950408889634
NO_COST = pl.CostEstimate(flops=0, bytes_accessed=0, transcendentals=0)


def elu(v):
    return jnp.where(v > 0, v, jnp.exp(jnp.minimum(v, 0.0)) - 1.0)


def dot(a, b):
    return jnp.dot(a, b, preferred_element_type=F32)


def in_vmem(n):
    return [pl.BlockSpec(memory_space=pltpu.VMEM)] * n


def params(mib):
    return pltpu.CompilerParams(vmem_limit_bytes=mib * 1024 * 1024)


def encoder_kernel(halo_ref, audio_ref, taps_ref, back_ref, down_ref, out_ref, u_ref, e_ref):
    u_ref[0:8, :] = jnp.zeros((8, CH), F32)
    u_ref[8:16, :] = elu(halo_ref[...].astype(F32))
    u_ref[16:, :] = elu(audio_ref[...].astype(F32))
    rows = audio_ref.shape[0] + 8
    inner = dot(u_ref[2 : 2 + rows, :].astype(BF), taps_ref[0])
    inner += dot(u_ref[5 : 5 + rows, :].astype(BF), taps_ref[1])
    inner += dot(u_ref[8 : 8 + rows, :].astype(BF), taps_ref[2])
    hidden = elu(inner).astype(BF)
    branch = dot(hidden, back_ref[...])
    first = (halo_ref[...].astype(F32) + branch[0:8]).astype(BF)
    first = elu(first.astype(F32)).astype(BF).astype(F32)
    rest = (audio_ref[...].astype(F32) + branch[8:]).astype(BF)
    rest = elu(rest.astype(F32)).astype(BF).astype(F32)
    for j in range(CH // 128):
        e_ref[j, 0:8, :] = first[:, j * 128 : (j + 1) * 128]
        e_ref[j, 8:, :] = rest[:, j * 128 : (j + 1) * 128]
    acc = jnp.zeros((BLOCK, CH), F32)
    for k in range(4):
        e = [e_ref[j, pl.ds(6 + k, BLOCK, stride=2), :].astype(BF) for j in range(CH // 128)]
        acc += dot(jnp.concatenate(e, axis=1), down_ref[k])
    out_ref[...] = acc.astype(BF)


def encoder(halo, audio, taps, back, down):
    return pl.pallas_call(
        encoder_kernel,
        in_specs=in_vmem(5),
        out_specs=pl.BlockSpec(memory_space=pltpu.VMEM),
        out_shape=jax.ShapeDtypeStruct((BLOCK, CH), BF),
        scratch_shapes=[pltpu.VMEM((528, CH), F32), pltpu.VMEM((CH // 128, 520, 128), F32)],
        compiler_params=params(12),
        cost_estimate=NO_COST,
    )(halo, audio, taps, back, down)


def swap(a, axis):
    return lax.ppermute(a, axis, SWAP)


def shift(a, by):
    return lax.ppermute(a, "x", [(i, (i + by) % 4) for i in range(4)])


def split_kernel(at_ref, w_ref, near_ref, far_ref, *outs):
    x = at_ref[3]
    for dx in range(4):
        lanes = pl.ds(pl.multiple_of(lax.rem(x + dx, 4) * 256, 256), 256)
        outs[dx][...] = w_ref[:, :, lanes]
    outs[4][0] = near_ref[...]
    outs[4][1] = far_ref[...]


def split(at, w, embed):
    whole = lambda shape: pl.BlockSpec(shape, lambda i, at: (0,) * len(shape))
    return pl.pallas_call(
        split_kernel,
        grid_spec=pltpu.PrefetchScalarGridSpec(
            num_scalar_prefetch=1,
            grid=(1,),
            in_specs=[
                whole((3, 32, 1024)),
                pl.BlockSpec((128, 256), lambda i, at: (at[2], at[0])),
                pl.BlockSpec((128, 256), lambda i, at: (at[2], at[1])),
            ],
            out_specs=[whole((3, 32, 256))] * 4 + [whole((2, 128, 256))],
        ),
        out_shape=[jax.ShapeDtypeStruct((3, 32, 256), BF)] * 4 + [jax.ShapeDtypeStruct((2, 128, 256), BF)],
    )(at, w, embed, embed)


def unused(after):
    return in_vmem(len(after))


def stack_kernel(n, *refs):
    for i in range(n):
        refs[-1][i] = refs[i][...]


def stack(parts, after=()):
    return pl.pallas_call(
        functools.partial(stack_kernel, len(parts)),
        in_specs=in_vmem(len(parts)) + unused(after),
        out_specs=pl.BlockSpec(memory_space=pltpu.VMEM),
        out_shape=jax.ShapeDtypeStruct((len(parts),) + parts[0].shape, parts[0].dtype),
        compiler_params=params(4),
        cost_estimate=NO_COST,
    )(*parts, *after)


def partial_kernel(at_ref, w00, w01, w10, w11, mine_ref, rest_ref, g0, g1, t0, t1, *refs):
    out_ref, w_ref = refs[-2:]
    x, core = at_ref[3], at_ref[4]
    for y, pair in enumerate(((w00, w01), (w10, w11))):
        for c, ref in enumerate(pair):
            for dx in range(4):
                row = lax.rem(x + 4 - dx, 4) * 64 + (core ^ c) * 32
                for j in range(3):
                    w_ref[y, pl.ds(pl.multiple_of(row, 32), 32), j * 256 : (j + 1) * 256] = ref[dx, j]
    part = None
    line = None
    for y, (gain_ref, table_ref) in enumerate(((g0, t0), (g1, t1))):
        w = w_ref[y]
        gain = gain_ref[...]
        embed = jnp.concatenate([mine_ref[y], rest_ref[y]], axis=0).astype(F32) * gain
        table = jnp.concatenate([table_ref[...], jnp.zeros((6, 256), F32)], axis=0) * gain
        high = table.astype(BF)
        low = (table - high.astype(F32)).astype(BF)
        a = dot(embed.astype(BF), w)
        b = dot(high, w) + dot(low, w)
        part = a if part is None else part + a
        line = b if line is None else line + b
    top = line.astype(BF).astype(F32)
    rem = line - top
    rows = [v[s : s + 1, k * 128 : (k + 1) * 128] for v in (top, rem) for s in range(2) for k in range(6)]
    tail = jnp.concatenate(rows + [jnp.zeros((8, 128), F32)], axis=0).astype(BF)
    for i in range(8):
        out_ref[i, :, 0:768] = part[i * 32 : (i + 1) * 32].astype(BF)
        out_ref[i, :, 768:896] = tail


def partial_weights(at, ws, mine, rest, gain, table, after):
    whole = lambda shape: pl.BlockSpec(shape, lambda i, at: (0,) * len(shape))
    here = lambda rows, k: pl.BlockSpec((rows, 256), lambda i, at: (0, at[k]))
    return pl.pallas_call(
        partial_kernel,
        grid_spec=pltpu.PrefetchScalarGridSpec(
            num_scalar_prefetch=1,
            grid=(1,),
            in_specs=[whole((4, 3, 32, 256))] * 4
            + [whole((2, 128, 256))] * 2
            + [here(1, 0), here(1, 1), here(2, 0), here(2, 1)]
            + unused(after),
            out_specs=whole((8, 32, 896)),
            scratch_shapes=[pltpu.VMEM((2, 256, 768), BF)],
        ),
        out_shape=jax.ShapeDtypeStruct((8, 32, 896), BF),
        compiler_params=params(10),
        cost_estimate=NO_COST,
    )(at, *ws, mine, rest, gain, gain, table, table, *after)


def sum_kernel(p_ref, *refs):
    m_ref, line_ref = refs[-2:]
    total = jnp.sum(p_ref[...].astype(F32), axis=0)
    m = total[:, :768].astype(BF)
    for i in range(8):
        m_ref[i] = m
    both = total[0:12, 768:] + total[12:24, 768:]
    line_ref[...] = jnp.zeros((8, 768), F32)
    for s in range(2):
        for k in range(6):
            line_ref[s : s + 1, k * 128 : (k + 1) * 128] = both[s * 6 + k : s * 6 + k + 1]


def sum_weights(packed, after):
    return pl.pallas_call(
        sum_kernel,
        in_specs=in_vmem(1) + unused(after),
        out_specs=in_vmem(2),
        out_shape=[jax.ShapeDtypeStruct((8, 32, 768), BF), jax.ShapeDtypeStruct((8, 768), F32)],
        compiler_params=params(8),
        cost_estimate=NO_COST,
    )(packed, *after)


def term_kernel(at_ref, latent_ref, embed_ref, *refs):
    give_ref, own_ref = refs[-2:]
    term = dot(latent_ref[...], embed_ref[...])
    mine = at_ref[5] == pl.program_id(0) // 2

    @pl.when(mine)
    def _():
        own_ref[...] = term.astype(BF)

    @pl.when(jnp.logical_not(mine))
    def _():
        give_ref[...] = term.astype(BF)


def terms(at, latent, embed, after):
    def give_at(i, at):
        return (0, jnp.where(at[5] == 0, jnp.maximum(i - 2, 0), jnp.minimum(i, 1)))

    def own_at(i, at):
        return (0, jnp.where(at[5] == 1, jnp.maximum(i - 2, 0), jnp.minimum(i, 1)))

    return pl.pallas_call(
        term_kernel,
        grid_spec=pltpu.PrefetchScalarGridSpec(
            num_scalar_prefetch=1,
            grid=(4,),
            in_specs=[pl.BlockSpec((BLOCK, CH), lambda i, at: (0, 0)), pl.BlockSpec((CH, 1024), lambda i, at: (0, i))]
            + unused(after),
            out_specs=[pl.BlockSpec((BLOCK, 1024), give_at), pl.BlockSpec((BLOCK, 1024), own_at)],
        ),
        out_shape=[jax.ShapeDtypeStruct((BLOCK, D // 2), BF)] * 2,
        compiler_params=params(10),
        cost_estimate=NO_COST,
    )(at, latent, embed, *after)


def embed_kernel(at_ref, own_ref, got_ref, active_ref, table_ref, *refs):
    out_ref, square_ref = refs[-2:]
    act = active_ref[:, pl.ds(at_ref[3] + 4, 1), :].reshape(2, BLOCK)
    cols = jnp.concatenate([act, jnp.zeros((6, BLOCK), F32)], axis=0).T
    x = own_ref[...].astype(F32) + got_ref[...].astype(F32)
    x = x + cols[:, 0:1] * table_ref[0:1] + cols[:, 1:2] * table_ref[1:2]
    out_ref[...] = x.astype(BF)
    square = jnp.sum(x * x, axis=1, keepdims=True)
    square = jnp.broadcast_to(square, (BLOCK, 128)).T[0:8]

    @pl.when(pl.program_id(0) == 0)
    def _():
        square_ref[...] = square

    @pl.when(pl.program_id(0) != 0)
    def _():
        square_ref[...] += square


def embed_rows(at, own, got, active, table, after):
    tile = pl.BlockSpec((BLOCK, 1024), lambda i, at: (0, i))
    return pl.pallas_call(
        embed_kernel,
        grid_spec=pltpu.PrefetchScalarGridSpec(
            num_scalar_prefetch=1,
            grid=(2,),
            in_specs=[
                tile,
                tile,
                pl.BlockSpec((2, 8, BLOCK), lambda i, at: (0, 0, 0)),
                pl.BlockSpec((2, 1024), lambda i, at: (0, at[5] * 2 + i)),
            ]
            + unused(after),
            out_specs=[tile, pl.BlockSpec((8, BLOCK), lambda i, at: (0, 0))],
        ),
        out_shape=[jax.ShapeDtypeStruct((BLOCK, D // 2), BF), jax.ShapeDtypeStruct((8, BLOCK), F32)],
        compiler_params=params(10),
        cost_estimate=pl.CostEstimate(flops=20000000000, bytes_accessed=0, transcendentals=0),
    )(at, own, got, active, table, *after)


def project_rows(row, blocks, m_ref, line_ref, active_ref, scale_ref, at_ref, kv_ref, q_ref):
    x = at_ref[3]
    cols = slice(0, 768) if q_ref is not None else slice(256, 768)
    w0, w1 = m_ref[0:512, cols], m_ref[512:1024, cols]
    line = line_ref[:, cols]
    for dx in range(4):
        at = lax.rem(x + dx, 4)
        act = active_ref[:, pl.ds(4 * row + at, 1), :].reshape(2, BLOCK)
        side = jnp.concatenate([act, scale_ref[pl.ds(at ^ x, 1), :], jnp.zeros((5, BLOCK), F32)], axis=0).T
        acc = dot(blocks[dx][0], w0) + dot(blocks[dx][1], w1)
        acc = (acc + side[:, 0:1] * line[0:1] + side[:, 1:2] * line[1:2]) * side[:, 2:3]
        kv_ref[at] = acc[:, -512:].astype(BF)
        if q_ref is not None:
            q_ref[at] = (acc[:, :256] * (HD**-0.5 * LOG2E)).astype(BF)


def project_own_kernel(at_ref, a, al, ar, af, m00, m01, m10, m11, line_ref, active_ref, scale_ref, kv_ref, q_ref, m_ref):
    core, yl = at_ref[4], at_ref[6]
    for y, pair in enumerate(((m00, m01), (m10, m11))):
        for c, ref in enumerate(pair):
            row = ((yl ^ y) * 2 + (core ^ c)) * 128
            for s in range(2):
                m_ref[pl.ds(pl.multiple_of(s * 512 + row, 128), 128), :] = ref[s * 128 : (s + 1) * 128, :]
    project_rows(1, (a, ar, af, al), m_ref, line_ref, active_ref, scale_ref, at_ref, kv_ref, q_ref)


def project_prev_kernel(at_ref, b, bl, br, bf, m_ref, line_ref, active_ref, scale_ref, kv_ref):
    project_rows(0, (b, br, bf, bl), m_ref, line_ref, active_ref, scale_ref, at_ref, kv_ref, None)


def project(kernel, outs, *args):
    return pl.pallas_call(
        kernel,
        in_specs=[pl.BlockSpec(memory_space=pltpu.SMEM)] + in_vmem(len(args) - 1),
        out_specs=in_vmem(len(outs)),
        out_shape=outs,
        compiler_params=params(10),
        cost_estimate=NO_COST,
    )(*args)


def attention_kernel(n, place_ref, q_ref, om_ref, ot_ref, pm_ref, pt_ref, *o_refs):
    x, core, first = place_ref[0], place_ref[1], place_ref[2]
    half = BLOCK // 2
    cols = lax.broadcasted_iota(jnp.int32, (half, BLOCK), 1)
    ones = jnp.ones((8 * BLOCK, HD), BF)
    contract = (((1,), (1,)), ((), ()))
    for step in range(n):
        at = lax.rem(x + place_ref[3 + step], 4)
        blocks, penalties = [], []
        for own_ref, prev_ref, begin in ((om_ref, pm_ref, at + 1), (ot_ref, pt_ref, at + core)):
            for j in range(4):
                m = begin + j
                i = lax.rem(m, 4)
                blocks.append(jnp.where(m >= 4, own_ref[i], prev_ref[i]))
                penalties.append(jnp.where((m < 4) & (first == 1), 1e30, 0.0))
        kv = jnp.concatenate(blocks, axis=0)
        for h in range(2):
            q = q_ref[at, :, h * HD : (h + 1) * HD]
            k = kv[:, h * HD : (h + 1) * HD]
            v = jnp.concatenate([kv[:, 256 + h * HD : 256 + (h + 1) * HD], ones], axis=1)
            for begin in (0, half):
                rows = lax.broadcasted_iota(jnp.int32, (half, BLOCK), 0) + begin
                s = lax.dot_general(q[begin : begin + half], k, contract, preferred_element_type=F32)
                s = [s[:, j * BLOCK : (j + 1) * BLOCK] for j in range(8)]
                s[3] = jnp.where(cols <= rows, s[3], -1e30)
                s[4] = jnp.where(cols > rows, s[4], -1e30)
                tops = [jnp.max(v, axis=1, keepdims=True) - penalty for v, penalty in zip(s, penalties)]
                top = functools.reduce(jnp.maximum, tops)
                p = [jnp.exp2(v - (top + penalty)).astype(BF) for v, penalty in zip(s, penalties)]
                o = dot(jnp.concatenate(p, axis=1), v)
                o_refs[step][begin : begin + half, h * HD : (h + 1) * HD] = (o[:, :HD] / o[:, HD:]).astype(BF)


def attention(place, offsets, *args):
    n = len(offsets)
    return pl.pallas_call(
        functools.partial(attention_kernel, n),
        in_specs=[pl.BlockSpec(memory_space=pltpu.SMEM)] + in_vmem(5),
        out_specs=in_vmem(n),
        out_shape=[jax.ShapeDtypeStruct((BLOCK, 256), BF)] * n,
        compiler_params=params(10),
        cost_estimate=NO_COST,
    )(jnp.concatenate([place, jnp.array(offsets, jnp.int32)]), *args)


def collect_kernel(place_ref, a_ref, b_ref, c_ref, d_ref, o_ref):
    for dx, ref in enumerate((a_ref, b_ref, c_ref, d_ref)):
        at = lax.rem(place_ref[0] + 4 - dx, 4)
        o_ref[:, pl.ds(pl.multiple_of(at * 256, 256), 256)] = ref[...]


def collect(place, parts):
    return pl.pallas_call(
        collect_kernel,
        in_specs=[pl.BlockSpec(memory_space=pltpu.SMEM)] + in_vmem(4),
        out_specs=pl.BlockSpec(memory_space=pltpu.VMEM),
        out_shape=jax.ShapeDtypeStruct((BLOCK, 1024), BF),
        compiler_params=params(12),
    )(place, *parts)


def on_device(
    audio_feats,
    res_conv,
    res_out,
    down_conv,
    stream_embed,
    turn_lengths,
    speaker_table,
    norm_gain,
    qkv_weight,
):
    tp = lax.axis_index("tp")
    x_at = lax.axis_index("x")
    core = lax.axis_index("c")
    yl = lax.axis_index("yl")
    z = lax.axis_index("z")
    row = yl * 8 + z
    at = jnp.stack([yl * 8 + z, (1 - yl) * 8 + z, yl * 2 + core, x_at, core, tp, yl]).astype(jnp.int32)
    behind = [(i, i + 1) for i in range(15)]

    audio = audio_feats[0]
    halo = lax.ppermute(audio[-8:], CTX, [(i, i + 1) for i in range(127)])
    embed = stream_embed[0]
    *chunks, mine = split(at, qkv_weight, embed)
    arrived = [shift(chunks[dx], dx) for dx in (1, 2, 3)]
    rest = swap(mine, "tp")

    latent = encoder(halo, audio, res_conv[0], res_out[0], down_conv[0])
    give, own = terms(at, latent, embed, ())
    other = swap(latent, "tp")
    a = stack([latent, other])
    prev = lax.ppermute(latent, ("yl", "z"), behind)
    b = stack([prev, lax.ppermute(other, ("yl", "z"), behind)])
    al, ar = shift(a, 1), shift(a, 3)
    bl, br = shift(b, 1), shift(b, 3)
    af, bf = shift(al, 1), shift(br, 3)

    w00 = stack([chunks[0]] + arrived, (latent, rest))
    w10 = swap(w00, "yl")
    w01 = swap(w00, "c")
    w11 = swap(w10, "c")
    packed = partial_weights(at, (w00, w01, w10, w11), mine, rest, norm_gain[None], speaker_table, (give, other, prev))
    packed = lax.all_to_all(packed, "z", 0, 0, tiled=True)
    m, lines = sum_weights(packed, ())
    bounds = jnp.cumsum(turn_lengths, axis=1)
    start = ((row - 1 + jnp.arange(2)[:, None]) * 8 + 2 * jnp.arange(4)[None, :] + core) * BLOCK
    frames = start.reshape(8, 1) + jnp.arange(BLOCK)
    turn = jnp.sum((bounds[:, :, None, None] <= frames[None, None]).astype(jnp.int32), axis=1)
    active = (turn % 2 == 1).astype(F32)

    got = swap(give, "tp")
    embedded, square = embed_rows(at, own, got, active, speaker_table, (al, ar, b))
    square = square[0:1]
    beside = lax.ppermute(square, "x", [(i, i ^ 1) for i in range(4)])
    across = lax.ppermute(square, ("x", "tp"), [(i, i ^ 3) for i in range(8)])
    square = jnp.concatenate([square + swap(square, "tp"), beside + across])
    scale = lax.rsqrt(square * (1.0 / D) + 1e-05)
    scales = jnp.concatenate([scale, lax.ppermute(scale, "x", [(i, i ^ 2) for i in range(4)])])
    m00 = lax.all_to_all(m, "z", 0, 0, tiled=True).reshape(256, 768)
    (m00,) = stack([m00], (scales, bl, br))
    m10 = swap(m00, "yl")
    m01 = swap(m00, "c")
    m11 = swap(m10, "c")
    scales_prev = lax.ppermute(scales, ("yl", "z"), behind)

    kv = jax.ShapeDtypeStruct((4, BLOCK, 512), BF)
    half = jax.ShapeDtypeStruct((4, BLOCK, 256), BF)
    full = jax.ShapeDtypeStruct((1024, 768), BF)
    om, q, whole = project(
        project_own_kernel, (kv, half, full), at, a, al, ar, af, m00, m01, m10, m11, lines, active, scales
    )
    ot = swap(om, "c")
    (pm,) = project(project_prev_kernel, (kv,), at, b, bl, br, bf, whole, lines, active, scales_prev)
    pt = swap(pm, "c")

    place = jnp.stack([x_at, core, (row == 0).astype(jnp.int32)]).astype(jnp.int32)
    blocks = (q, om, ot, pm, pt)
    sent = (2, 1, 3)
    parts = dict(zip(sent, attention(place, sent, *blocks)))
    parts = {dx: shift(part, dx) for dx, part in parts.items()}
    (parts[0],) = attention(place, (0,), *blocks)
    return embedded, collect(place, [parts[dx] for dx in range(4)])


def solution(mesh):
    fine = Mesh(mesh.devices.reshape(2, 8, 4, 2, 2), CTX + ("tp",))
    placed = (
        P("tp", CTX, None),
        P("tp", None, None, None),
        P("tp", None, None),
        P("tp", None, None, None),
        P("tp", None, None),
        P(),
        P(),
        P(),
        P(None, CTX, "tp"),
    )
    return jax.shard_map(
        on_device,
        mesh=fine,
        in_specs=placed,
        out_specs=(P(CTX, "tp"), P(CTX, "tp")),
        check_vma=False,
    )
```
